512 devices in a mesh: dp: 64 (over z_lo, y, core), tensor: 8 (over z_hi, x).
Axes of the slice: x: 4, y: 4, z: 16 (z_hi: 2, z_lo: 8; z = z_hi * 8 + z_lo), core: 2. Of those that a mesh axis runs over, the one named last changes fastest.
Arguments:
- activation: bfloat16 [24576, 6656], P('dp', 'tensor'), may hold values from -6 to 6
- w_query: bfloat16 [6656, 1024], P(None, 'tensor'), may hold values from -0.5 to 0.5
- key_rows: bfloat16 [24576, 1024], P('dp', 'tensor'), may hold values from -8 to 8
- value_rows: bfloat16 [24576, 1024], P('dp', 'tensor'), may hold values from -6 to 6
- out_grad: bfloat16 [24576, 1024], P('dp', 'tensor'), may hold values from -6 to 6
- owners: int32 [8, 52, 1], P('tensor'), may hold values from 0 to 63; in each aligned block of 52 rows (0 to 51, 52 to 103, ..., all dimensions but the last counted through in order) at most 2 rows name the same one
- master_copy: float32 [128, 128, 1024], P('dp', None, 'tensor'), may hold values from -0.078125 to 0.078125
- first_moment: float32 [128, 128, 1024], P('dp', None, 'tensor'), may hold values from -4 to 4
- second_moment: float32 [128, 128, 1024], P('dp', None, 'tensor'), may hold values from 0.01 to 1
Outputs:
- new_weights: bfloat16 [6656, 1024], P(None, 'tensor')
- new_master: float32 [128, 128, 1024], P('dp', None, 'tensor')
- new_first: float32 [128, 128, 1024], P('dp', None, 'tensor')
- new_second: float32 [128, 128, 1024], P('dp', None, 'tensor')
The draws below stay inside these ranges and needn't reach their ends.
Inputs may be any that keep to these rules, and one draw needn't show every extreme that they name: `owners`: within one head no dp index owns more than 2 blocks, one owns exactly 2; every dp index owns some block of some head.
All inputs are finite; a program needn't handle non-finite values.
Results may differ from the reference program's by a relative error of at most 0.0055.
The reference program's roundings to bfloat16 on the way (of `queries`, `dscores` and `dquery`) count: a program that leaves them out, or rounds other values in their place, can miss the bound.
Values may be sent and summed in bfloat16 or wider, within the bound.
A program may use at most 64 MiB of HBM per device.

```python
import math
import jax
import jax.numpy as jnp
import numpy as np
from jax import lax

D = 6656
HD = 128
RB = 128
TOK_DEV = 384
HEADS = 8
NBLK = 52
CAP = 2
TOKENS = 24576
N_DP = 64


def draw_activation(key, part):
    key = jax.random.fold_in(key, 3)
    values = jax.random.truncated_normal(key, -6.0, 6.0, (TOKENS, D), jnp.float32)
    return values.astype(jnp.bfloat16)


def draw_w_query(key, part):
    key = jax.random.fold_in(key, 5)
    values = jax.random.truncated_normal(key, -6.0, 6.0, (D, HEADS * HD), jnp.float32) * D ** (-0.5)
    return values.astype(jnp.bfloat16)


def draw_key_rows(key, part):
    key = jax.random.fold_in(key, 7)
    values = jax.random.truncated_normal(key, -6.0, 6.0, (TOKENS, HEADS * HD), jnp.float32)
    return values.astype(jnp.bfloat16)


def steps_of(own_key, shape, split, least, high):
    def one(dim, blocks):
        heights = jax.random.uniform(jax.random.fold_in(jax.random.fold_in(own_key, 6), dim), (blocks,), jnp.float32, least / len(split), high / len(split))
        return jnp.repeat(jnp.exp(heights), shape[dim] // blocks).reshape((-1,) + (1,) * (len(shape) - dim - 1))

    loudness = one(*split[0])
    for cut in split[1:]:
        loudness = loudness * one(*cut)
    return loudness


def shared_out(stream_key, own, number, rows, amount, top, most, lean):
    sequence = jax.random.permutation(stream_key, amount)
    crowded, usual = portions_of(amount, rows * top, most, lean, True), portions_of(amount, rows * top, most, lean, False)
    places = jnp.arange(amount)

    def named(tallies, offset_by):
        used = int((tallies > 0).sum())
        fixed = max(1, used // 4)
        moved = fixed + (places - fixed + offset_by * (used - fixed)) % max(1, amount - fixed)
        return jnp.zeros((amount,), jnp.int32).at[sequence[jnp.where(places < fixed, places, moved)]].set(jnp.asarray(tallies, jnp.int32))

    tallies = jnp.where(number % 4 == 0, named(crowded, number // 4), named(usual, number - number // 4 - 1))
    mixed = jax.random.permutation(jax.random.fold_in(own, 3), amount)
    source_of, sink = mixed[0:amount // 2 * 2:2], mixed[1:amount // 2 * 2:2]
    margin = jnp.minimum(tallies[source_of] - 1, most - tallies[sink]) // 2
    margin = jnp.where((source_of == sequence[0]) | (sink == sequence[0]) | (tallies[sink] == 0), 0, jnp.maximum(margin, 0))
    moved = jax.random.randint(jax.random.fold_in(own, 4), (amount // 2,), 0, 1 << 20) % (margin + 1)
    tallies = tallies.at[source_of].add(-moved).at[sink].add(moved)
    labels = jnp.searchsorted(jnp.cumsum(tallies), jnp.arange(rows * top), side="right").astype(jnp.int32)
    listing = labels.reshape(top, rows).T
    listing = listing[jax.random.permutation(jax.random.fold_in(own, 1), rows)]
    offset_by = jax.random.randint(jax.random.fold_in(own, 2), (rows, 1), 0, top)
    return jnp.take_along_axis(listing, (jnp.arange(top)[None, :] + offset_by) % top, axis=1)


def portions_of(amount, total, bound, lean, full):
    weights = [(1 << 20) // math.isqrt(grade ** lean) + 1 for grade in range(1, amount + 1)]
    largest = bound if full else min(bound, max(-(-total // amount), total * weights[0] // sum(weights)))
    least = 1 if total - largest >= amount - 1 else 0
    given, rest = [largest] + [least] * (amount - 1), total - largest - least * (amount - 1)
    while rest > 0:
        candidates = [i for i in range(1, amount) if given[i] < largest] or [i for i in range(1, amount) if given[i] < bound]
        pool, remaining = sum([weights[i] for i in candidates]), rest
        for i in candidates:
            addition = min(bound - given[i], max(1, remaining * weights[i] // pool), rest)
            given[i] = given[i] + addition
            rest = rest - addition
    return np.array(given)


def bell_draw(rng, dims, width, most, split=(), held_as=jnp.bfloat16):
    loudness = steps_of(rng, dims, split, -0.22, 0.18) if split else 1.0
    entries = jax.random.normal(rng, dims, jnp.float32) * width * loudness
    return jnp.minimum(jnp.maximum(entries, -most), most).astype(held_as)


def setup_inputs(seed: int = 0) -> dict:
    splits = jax.random.split(jax.random.key(seed), 10)
    activation = draw_activation(jax.random.fold_in(splits[9], 71), 0)
    w_query = draw_w_query(jax.random.fold_in(splits[9], 71), 0)
    key_rows = draw_key_rows(jax.random.fold_in(splits[9], 71), 0)
    value_rows = bell_draw(splits[3], (TOKENS, HEADS * HD), 1.0, 6.0, ((0, 64), (1, 8)))
    out_grad = bell_draw(splits[4], (TOKENS, HEADS * HD), 1.0, 6.0, ((0, 64), (1, 8)))
    owners_keys = jax.random.split(jax.random.fold_in(splits[5], 1), HEADS * NBLK // NBLK)
    owners_turns = jax.random.permutation(jax.random.fold_in(splits[5], 3), HEADS * NBLK // NBLK)
    owners = jax.vmap(lambda own, number: shared_out(jax.random.fold_in(splits[5], 2), own, number, NBLK, N_DP, 1, CAP, 2))(owners_keys, owners_turns).reshape((HEADS, NBLK, 1))
    master_copy = bell_draw(splits[6], (N_DP * CAP, RB, HEADS * HD), D ** -0.5, 0.078125, ((0, 64), (2, 8)), jnp.float32)
    first_moment = bell_draw(splits[7], (N_DP * CAP, RB, HEADS * HD), 0.5, 4.0, ((0, 64), (2, 8)), jnp.float32)
    second_moment = jnp.clip(jnp.exp(math.log(1.0) - 4.6051702 * jax.random.uniform(splits[8], (N_DP * CAP, RB, HEADS * HD), jnp.float32) ** steps_of(splits[8], (N_DP * CAP, RB, HEADS * HD), ((0, 64), (2, 8)), -0.2, 0.2)), 0.01, 1.0)
    return {"activation": activation, "w_query": w_query, "key_rows": key_rows, "value_rows": value_rows, "out_grad": out_grad, "owners": owners, "master_copy": master_copy, "first_moment": first_moment, "second_moment": second_moment}


beta_first = 0.9
beta_second = 0.95
learn_rate = 0.001
adam_eps = 1e-08
adam_step = 100.0

def block_slots(own_row, capacity):
    count = own_row.shape[0]
    order = jnp.arange(count, dtype=jnp.int32)
    earlier = (own_row[:, None] == own_row[None, :]) & (order[:, None] < order[None, :])
    position = lax.optimization_barrier(jnp.sum(earlier.astype(jnp.int32), axis=0))
    return (own_row * capacity + position).astype(jnp.int32)

def attend_back(tokens, w_head, key_part, value_part, grad_part):
    factor = HD ** (-0.5)
    queries = jnp.dot(tokens, w_head, preferred_element_type=jnp.float32).astype(jnp.bfloat16)
    scores = jnp.dot(queries, key_part.T, preferred_element_type=jnp.float32) * factor
    length = scores.shape[0]
    row_pos = jnp.arange(length)[:, None]
    col_pos = jnp.arange(length)[None, :]
    scores = jnp.where(row_pos >= col_pos, scores, -1e+30)
    shifted = jnp.exp(scores - lax.optimization_barrier(jnp.max(scores, axis=1, keepdims=True)))
    attention = shifted / lax.optimization_barrier(jnp.sum(shifted, axis=1, keepdims=True))
    rounded = attention.astype(jnp.bfloat16)
    outputs = jnp.dot(rounded, value_part, preferred_element_type=jnp.float32)
    deltas = lax.optimization_barrier(jnp.sum(grad_part.astype(jnp.float32) * outputs, axis=1, keepdims=True))
    upstream = jnp.dot(grad_part, value_part.T, preferred_element_type=jnp.float32)
    dscores = (attention * (upstream - deltas)).astype(jnp.bfloat16)
    dquery = (jnp.dot(dscores, key_part, preferred_element_type=jnp.float32) * factor).astype(jnp.bfloat16)
    return jnp.dot(tokens.T, dquery, preferred_element_type=jnp.float32)

def adam_update(gradient, master, first, second, used):
    first_new = beta_first * first + (1.0 - beta_first) * gradient
    second_new = beta_second * second + (1.0 - beta_second) * gradient * gradient
    corr_first = 1.0 - beta_first ** adam_step
    corr_second = 1.0 - beta_second ** adam_step
    master_new = master - learn_rate * (first_new / corr_first) / (jnp.sqrt(second_new / corr_second) + adam_eps)
    return (master_new * used, first_new * used, second_new * used)

def reference(activation, w_query, key_rows, value_rows, out_grad, owners, master_copy, first_moment, second_moment):
    sequences = activation.reshape(N_DP, TOK_DEV, D)
    weight_cols, master_cols, first_cols, second_cols = ([], [], [], [])
    for head in range(HEADS):
        lower = head * HD
        w_head = w_query[:, lower:lower + HD]
        key_head = key_rows[:, lower:lower + HD].reshape(N_DP, TOK_DEV, HD)
        value_head = value_rows[:, lower:lower + HD].reshape(N_DP, TOK_DEV, HD)
        grad_head = out_grad[:, lower:lower + HD].reshape(N_DP, TOK_DEV, HD)

        def add_sequence(carry, pieces):
            return (carry + attend_back(pieces[0], w_head, pieces[1], pieces[2], pieces[3]), None)
        gradient, _ = lax.scan(add_sequence, jnp.zeros((D, HD), jnp.float32), (sequences, key_head, value_head, grad_head))
        target = block_slots(owners[head, :, 0], CAP)
        blocks = gradient.reshape(NBLK, RB, HD)
        slot_grad = jnp.zeros((N_DP * CAP, RB, HD), jnp.float32).at[target].set(blocks)
        used = jnp.zeros((N_DP * CAP,), jnp.float32).at[target].set(1.0)[:, None, None]
        master_new, first_new, second_new = adam_update(slot_grad, master_copy[:, :, lower:lower + HD], first_moment[:, :, lower:lower + HD], second_moment[:, :, lower:lower + HD], used)
        weight_cols.append(master_new.astype(jnp.bfloat16)[target].reshape(D, HD))
        master_cols.append(master_new)
        first_cols.append(first_new)
        second_cols.append(second_new)
    return (jnp.concatenate(weight_cols, axis=1), jnp.concatenate(master_cols, axis=2), jnp.concatenate(first_cols, axis=2), jnp.concatenate(second_cols, axis=2))
```

```python
import functools

import jax
import jax.numpy as jnp
from jax import lax
from jax.experimental import pallas as pl
from jax.experimental.pallas import tpu as pltpu
from jax.sharding import PartitionSpec as P

beta_first = 0.9
beta_second = 0.95
learn_rate = 0.001
adam_eps = 1e-08
adam_step = 100.0

MESH = pl.DeviceIdType.MESH
TOK = 384
FEAT = 832
HD = 128
NBLK = 52
HALF = 26
SUB = 16
UNITS = 13
CHUNKS = 3
CTOK = TOK // CHUNKS


def adam_update(gradient, master, first, second, used):
    first_new = beta_first * first + (1.0 - beta_first) * gradient
    second_new = beta_second * second + (1.0 - beta_second) * gradient * gradient
    corr_first = 1.0 - beta_first**adam_step
    corr_second = 1.0 - beta_second**adam_step
    master_new = master - learn_rate * (first_new / corr_first) / (
        jnp.sqrt(second_new / corr_second) + adam_eps
    )
    return (master_new * used, first_new * used, second_new * used)


def dot_t(a, b):
    return lax.dot_general(a, b, (((1,), (1,)), ((), ())), preferred_element_type=jnp.float32)


def dot_0(a, b):
    return lax.dot_general(a, b, (((0,), (0,)), ((), ())), preferred_element_type=jnp.float32)


def kernel(
    block_of, used_of, slot_of,
    act, w, keys, values, outg, master, first, second,
    out_w, out_m, out_f, out_s,
    whole, sib, qacc, dq, grad, recv_y, gsum, recv_z, gall, send_g, recv_g, send_w, recv_w, wall,
    z_s, z_r, x_s, x_r, f_s, f_r, s_s, s_r, d_s, d_r, y_s, y_r, r_s, r_r, a_s, a_r,
    o_s, o_r, b_s, b_r, w_s, w_r, v_s, v_r, c_s, c_r, l_sem,
):
    dp = lax.axis_index("dp")
    t = lax.axis_index("tensor")
    zl = dp // 8
    part = lax.rem(dp, 8)
    y = part // 2
    c = lax.rem(part, 2)
    a = t // 4
    x = lax.rem(t, 4)

    def at_x(d):
        return (dp, a * 4 + lax.rem(x + d, 4))

    opposite = (dp, (1 - a) * 4 + x)
    sibling = (zl * 8 + y * 2 + (1 - c), t)

    def at_part(p):
        return (zl * 8 + p, t)

    def at_z(z):
        return (z * 8 + part, t)

    barrier = pltpu.get_barrier_semaphore()
    peers = [at_x(d) for d in (1, 2, 3)] + [opposite]
    peers += [at_part(lax.rem(part + d, 8)) for d in range(1, 8)]
    peers += [at_z(lax.rem(zl + d, 8)) for d in range(1, 8)]
    for peer in peers:
        pl.semaphore_signal(barrier, inc=1, device_id=peer, device_id_type=MESH)
    pl.semaphore_wait(barrier, len(peers))

    def remote(src, dst, ss, rs, dev):
        return pltpu.make_async_remote_copy(
            src_ref=src, dst_ref=dst, send_sem=ss, recv_sem=rs, device_id=dev, device_id_type=MESH
        )

    own = pltpu.make_async_copy(act, whole.at[t], l_sem)
    own.start()
    rows = [pl.ds(i * CTOK, CTOK) for i in range(CHUNKS)]
    cross = [
        remote(act.at[r], whole.at[t, r], z_s.at[i], z_r.at[i], opposite) for i, r in enumerate(rows)
    ]
    for cp in cross:
        cp.start()
    along = []
    for i, r in enumerate(rows):
        for d in (1, 3, 2):
            cp = remote(act.at[r], whole.at[t, r], x_s.at[d - 1, i], x_r.at[d - 1, i], at_x(d))
            cp.start()
            along.append(cp)
    t_op = (1 - a) * 4 + x
    onward = []
    for i, r in enumerate(rows):
        cross[i].wait_recv()
        for d in (1, 3, 2):
            cp = remote(whole.at[t_op, r], whole.at[t_op, r], f_s.at[d - 1, i], f_r.at[d - 1, i], at_x(d))
            cp.start()
            onward.append(cp)
    own.wait()
    for cp in along:
        cp.wait_recv()
    for cp in onward:
        cp.wait_recv()
    share = []
    for j in range(4):
        cp = remote(whole.at[(1 - c) * 4 + j], sib.at[j], s_s.at[j], s_r.at[j], sibling)
        cp.start()
        share.append(cp)

    qacc[...] = jnp.zeros_like(qacc)

    def add_q(k, carry):
        qacc[...] += jnp.dot(whole[k], w[k], preferred_element_type=jnp.float32)
        return carry

    lax.fori_loop(0, 8, add_q, 0)
    factor = HD ** (-0.5)
    for i in range(CHUNKS):
        n = (i + 1) * CTOK
        r = rows[i]
        kk = keys[pl.ds(0, n)]
        vv = values[pl.ds(0, n)]
        og = outg[r]
        scores = dot_t(qacc[r].astype(jnp.bfloat16), kk) * factor
        row_pos = lax.broadcasted_iota(jnp.int32, (CTOK, n), 0) + i * CTOK
        col_pos = lax.broadcasted_iota(jnp.int32, (CTOK, n), 1)
        scores = jnp.where(row_pos >= col_pos, scores, -1e30)
        shifted = jnp.exp(scores - jnp.max(scores, axis=1, keepdims=True))
        attention = shifted / jnp.sum(shifted, axis=1, keepdims=True)
        outputs = jnp.dot(attention.astype(jnp.bfloat16), vv, preferred_element_type=jnp.float32)
        deltas = jnp.sum(og.astype(jnp.float32) * outputs, axis=1, keepdims=True)
        upstream = dot_t(og, vv)
        dscores = (attention * (upstream - deltas)).astype(jnp.bfloat16)
        dquery = jnp.dot(dscores, kk, preferred_element_type=jnp.float32) * factor
        dq[0, r] = dquery.astype(jnp.bfloat16)
    swap = remote(dq.at[0], dq.at[1], d_s, d_r, sibling)
    swap.start()
    swap.wait_recv()
    for cp in share:
        cp.wait_recv()
    for j in range(4):
        g = dot_0(whole[c * 4 + j], dq[0]) + dot_0(sib[j], dq[1])
        for m in range(13):
            k = j * 13 + m
            grad[k // 2, k % 2] = g[m * 64 : (m + 1) * 64]

    to_parts = []
    for d in range(1, 8):
        p = lax.rem(part + d, 8)
        src = grad.at[:, p // 4, pl.ds(pl.multiple_of(lax.rem(p, 4) * SUB, SUB), SUB)]
        cp = remote(src, recv_y.at[part], y_s.at[d - 1], y_r.at[d - 1], at_part(p))
        cp.start()
        to_parts.append(cp)
    recv_y[part] = grad[:, part // 4, pl.ds(pl.multiple_of(lax.rem(part, 4) * SUB, SUB), SUB)]
    for cp in to_parts:
        cp.wait_recv()

    def add_y(k, carry):
        for h in range(2):
            total = recv_y[h, k] + recv_y[2 + h, k] + recv_y[4 + h, k] + recv_y[6 + h, k]
            gsum[pl.ds((h * HALF + k) * 2, 2)] = total.reshape(2, 8, HD)
        return carry

    lax.fori_loop(0, HALF, add_y, 0)

    def piece(z):
        return pl.ds(z * UNITS, UNITS)

    to_z = []
    for d in range(1, 8):
        z = lax.rem(zl + d, 8)
        cp = remote(gsum.at[piece(z)], recv_z.at[zl], r_s.at[d - 1], r_r.at[d - 1], at_z(z))
        cp.start()
        to_z.append(cp)
    recv_z[zl] = gsum[piece(zl)]
    for cp in to_z:
        cp.wait_recv()
    total = recv_z[0]
    for z in range(1, 8):
        total = total + recv_z[z]
    gall[piece(zl)] = total
    back_z = []
    for d in range(1, 8):
        z = lax.rem(zl + d, 8)
        cp = remote(gall.at[piece(zl)], gall.at[piece(zl)], a_s.at[d - 1], a_r.at[d - 1], at_z(z))
        cp.start()
        back_z.append(cp)
    for cp in back_z:
        cp.wait_recv()

    for p in range(8):
        for j in range(2):
            k = block_of[zl * 16 + p * 2 + j]
            send_g[p, j, 0:8] = gall[k * 2]
            send_g[p, j, 8:16] = gall[k * 2 + 1]
    to_owner = []
    for d in range(1, 8):
        p = lax.rem(part + d, 8)
        cp = remote(send_g.at[p], recv_g.at[part], o_s.at[d - 1], o_r.at[d - 1], at_part(p))
        cp.start()
        to_owner.append(cp)
    recv_g[part] = send_g[part]
    for cp in to_owner:
        cp.wait_recv()
    for j in range(2):
        used = used_of[dp * 2 + j]
        for p in range(8):
            r = pl.ds(p * SUB, SUB)
            nm, nf, ns = adam_update(recv_g[p, j], master[j, r], first[j, r], second[j, r], used)
            out_m[j, r] = nm
            out_f[j, r] = nf
            out_s[j, r] = ns
            send_w[p, j] = nm.astype(jnp.bfloat16)

    to_rows = []
    for d in range(1, 8):
        p = lax.rem(part + d, 8)
        cp = remote(send_w.at[p], recv_w.at[pl.ds(part * 2, 2)], b_s.at[d - 1], b_r.at[d - 1], at_part(p))
        cp.start()
        to_rows.append(cp)
    recv_w[pl.ds(part * 2, 2)] = send_w[part]
    for cp in to_rows:
        cp.wait_recv()
    wall[pl.ds(zl * 16, 16)] = recv_w[...]
    all_z = []
    for d in range(1, 8):
        z = lax.rem(zl + d, 8)
        cp = remote(recv_w, wall.at[pl.ds(zl * 16, 16)], w_s.at[d - 1], w_r.at[d - 1], at_z(z))
        cp.start()
        all_z.append(cp)
    for cp in all_z:
        cp.wait_recv()
    mine = pl.ds(pl.multiple_of(part * SUB, SUB), SUB)

    def place(k, carry):
        out_w[k, mine] = wall[slot_of[k]]
        return carry

    lax.fori_loop(0, NBLK, place, 0)
    to_y = []
    for d in (1, 3, 2):
        p = lax.rem(y + d, 4) * 2 + c
        cp = remote(out_w.at[:, mine], out_w.at[:, mine], v_s.at[d - 1], v_r.at[d - 1], at_part(p))
        cp.start()
        to_y.append(cp)
    to_core = [remote(out_w.at[:, mine], out_w.at[:, mine], c_s.at[0], c_r.at[0], sibling)]
    to_core[0].start()
    for n, d in enumerate((1, 3, 2)):
        to_y[n].wait_recv()
        p = lax.rem(y - d + 4, 4) * 2 + c
        r = pl.ds(pl.multiple_of(p * SUB, SUB), SUB)
        cp = remote(out_w.at[:, r], out_w.at[:, r], c_s.at[d], c_r.at[d], sibling)
        cp.start()
        to_core.append(cp)
    for cp in to_core:
        cp.wait_recv()
    sent = cross + along + onward + share + [swap] + to_parts + to_z + back_z
    for cp in sent + to_owner + to_rows + all_z + to_y + to_core:
        cp.wait_send()


def body(
    activation, w_query, key_rows, value_rows, out_grad, owners, master_copy, first_moment, second_moment
):
    own_row = owners[0, :, 0]
    order = jnp.arange(NBLK, dtype=jnp.int32)
    earlier = (own_row[:, None] == own_row[None, :]) & (order[:, None] < order[None, :])
    target = own_row * 2 + jnp.sum(earlier.astype(jnp.int32), axis=0)
    match = target[None, :] == jnp.arange(128, dtype=jnp.int32)[:, None]
    block_of = jnp.sum(jnp.where(match, order[None, :], 0), axis=1)
    used_of = jnp.sum(match.astype(jnp.float32), axis=1)
    smem = pl.BlockSpec(memory_space=pltpu.SMEM)
    vmem = pl.BlockSpec(memory_space=pltpu.VMEM)
    f32 = jnp.float32
    bf16 = jnp.bfloat16
    dma = pltpu.SemaphoreType.DMA
    new_w, new_m, new_f, new_s = pl.pallas_call(
        kernel,
        out_shape=(
            jax.ShapeDtypeStruct((NBLK, 128, HD), bf16),
            jax.ShapeDtypeStruct((2, 128, HD), f32),
            jax.ShapeDtypeStruct((2, 128, HD), f32),
            jax.ShapeDtypeStruct((2, 128, HD), f32),
        ),
        in_specs=[smem] * 3 + [vmem] * 8,
        out_specs=(vmem,) * 4,
        scratch_shapes=[
            pltpu.VMEM((8, TOK, FEAT), bf16),
            pltpu.VMEM((4, TOK, FEAT), bf16),
            pltpu.VMEM((TOK, HD), f32),
            pltpu.VMEM((2, TOK, HD), bf16),
            pltpu.VMEM((HALF, 2, 64, HD), f32),
            pltpu.VMEM((8, HALF, SUB, HD), f32),
            pltpu.VMEM((8 * UNITS, 8, HD), f32),
            pltpu.VMEM((8, UNITS, 8, HD), f32),
            pltpu.VMEM((8 * UNITS, 8, HD), f32),
            pltpu.VMEM((8, 2, SUB, HD), f32),
            pltpu.VMEM((8, 2, SUB, HD), f32),
            pltpu.VMEM((8, 2, SUB, HD), bf16),
            pltpu.VMEM((16, SUB, HD), bf16),
            pltpu.VMEM((128, SUB, HD), bf16),
            dma((CHUNKS,)), dma((CHUNKS,)),
            dma((3, CHUNKS)), dma((3, CHUNKS)),
            dma((3, CHUNKS)), dma((3, CHUNKS)),
            dma((4,)), dma((4,)),
            dma, dma,
            dma((7,)), dma((7,)),
            dma((7,)), dma((7,)),
            dma((7,)), dma((7,)),
            dma((7,)), dma((7,)),
            dma((7,)), dma((7,)),
            dma((7,)), dma((7,)),
            dma((3,)), dma((3,)),
            dma((4,)), dma((4,)),
            dma,
        ],
        compiler_params=pltpu.CompilerParams(
            collective_id=0, has_side_effects=True, vmem_limit_bytes=56 * 2**20
        ),
        name="project_back",
    )(
        block_of, used_of, target,
        activation, w_query.reshape(8, FEAT, HD), key_rows, value_rows, out_grad,
        master_copy, first_moment, second_moment,
    )
    return (new_w.reshape(NBLK * 128, HD), new_m, new_f, new_s)


def solution(mesh):
    return jax.shard_map(
        body,
        mesh=mesh,
        in_specs=(
            P("dp", "tensor"),
            P(None, "tensor"),
            P("dp", "tensor"),
            P("dp", "tensor"),
            P("dp", "tensor"),
            P("tensor", None, None),
            P("dp", None, "tensor"),
            P("dp", None, "tensor"),
            P("dp", None, "tensor"),
        ),
        out_specs=(
            P(None, "tensor"),
            P("dp", None, "tensor"),
            P("dp", None, "tensor"),
            P("dp", None, "tensor"),
        ),
        check_vma=False,
    )
```

```python
import functools

import jax
import jax.numpy as jnp
from jax import lax
from jax.experimental import pallas as pl
from jax.experimental.pallas import tpu as pltpu
from jax.sharding import PartitionSpec as P

beta_first = 0.9
beta_second = 0.95
learn_rate = 0.001
adam_eps = 1e-08
adam_step = 100.0

MESH = pl.DeviceIdType.MESH
TOK = 384
FEAT = 832
HD = 128
NBLK = 52
HALF = 26
HROWS = HALF * 128
SUB = 16
OWN = 7
PAD = 8 * OWN
CHUNKS = 3
CTOK = TOK // CHUNKS
LEVELS = 32700.0
FIXED = 32766.0
TOP_MASTER = 0.078125
TOP_FIRST = 4.0
TOP_SECOND = 1.0


def adam_update(gradient, master, first, second, used):
    first_new = beta_first * first + (1.0 - beta_first) * gradient
    second_new = beta_second * second + (1.0 - beta_second) * gradient * gradient
    corr_first = 1.0 - beta_first**adam_step
    corr_second = 1.0 - beta_second**adam_step
    master_new = master - learn_rate * (first_new / corr_first) / (
        jnp.sqrt(second_new / corr_second) + adam_eps
    )
    return (master_new * used, first_new * used, second_new * used)


def dot_t(a, b):
    return lax.dot_general(a, b, (((1,), (1,)), ((), ())), preferred_element_type=jnp.float32)


def dot_0(a, b):
    return lax.dot_general(a, b, (((0,), (0,)), ((), ())), preferred_element_type=jnp.float32)


def pack(v, inv):
    q = jnp.round(v * inv).astype(jnp.int32)
    return (q[:8] << 16) | (q[8:] & 0xFFFF)


def unpack(u, step):
    return jnp.concatenate([u >> 16, (u << 16) >> 16], axis=0).astype(jnp.float32) * step


def level(top):
    bits = jnp.log(jnp.maximum(top, 1e-30)) * (8.0 / 0.6931471805599453)
    return jnp.ceil(bits).astype(jnp.int32)


def step_of(e):
    return jnp.exp(e.astype(jnp.float32) * (0.6931471805599453 / 8.0)) * (1.0 / LEVELS)


def inverse_of(e):
    return jnp.exp(e.astype(jnp.float32) * (-0.6931471805599453 / 8.0)) * LEVELS


def kernel(
    slot_code, block_code,
    act, w, keys, values, outg, master, first, second,
    out_w, out_m, out_f, out_s,
    whole, sib, wt, dq, grad, ys, yr, gsum, zs, zr, red, gq, sys, syr, szs, szr, send_g, recv_g,
    z_s, z_r, x_s, x_r, f_s, f_r, s_s, s_r, d_s, d_r, y_s, y_r, r_s, r_r, a_s, a_r,
    o_s, o_r, w_s, w_r, v_s, v_r, c_s, c_r, k_s, k_r, p_s, p_r, l_sem,
):
    dp = lax.axis_index("dp")
    t = lax.axis_index("tensor")
    zl = dp // 8
    part = lax.rem(dp, 8)
    y = part // 2
    c = lax.rem(part, 2)
    a = t // 4
    x = lax.rem(t, 4)
    f32 = jnp.float32

    def at_x(d):
        return (dp, a * 4 + lax.rem(x + d, 4))

    opposite = (dp, (1 - a) * 4 + x)
    sibling = (zl * 8 + y * 2 + (1 - c), t)

    def at_part(p):
        return (zl * 8 + p, t)

    def at_z(z):
        return (z * 8 + part, t)

    barrier = pltpu.get_barrier_semaphore()
    peers = [at_x(d) for d in (1, 2, 3)] + [opposite]
    peers += [at_part(lax.rem(part + d, 8)) for d in range(1, 8)]
    peers += [at_z(lax.rem(zl + d, 8)) for d in range(1, 8)]
    for peer in peers:
        pl.semaphore_signal(barrier, inc=1, device_id=peer, device_id_type=MESH)
    pl.semaphore_wait(barrier, len(peers))
    sent = []

    def go(src, dst, ss, rs, dev):
        cp = pltpu.make_async_remote_copy(
            src_ref=src, dst_ref=dst, send_sem=ss, recv_sem=rs, device_id=dev, device_id_type=MESH
        )
        cp.start()
        sent.append(cp)
        return cp

    def rows(start, n, unit):
        return pl.ds(pl.multiple_of(start, unit), n)

    cols = [pl.ds(i * CTOK, CTOK) for i in range(CHUNKS)]
    mine = rows(t * FEAT, FEAT, 16)
    own = pltpu.make_async_copy(act, whole.at[mine], l_sem)
    own.start()
    cross = []
    for i in range(CHUNKS):
        for s in range(2):
            cross.append(
                go(
                    act.at[pl.ds(s * 416, 416), cols[i]],
                    whole.at[rows(t * FEAT + s * 416, 416, 16), cols[i]],
                    z_s.at[i, s], z_r.at[i, s], opposite,
                )
            )
    along = [
        [
            go(act.at[:, cols[i]], whole.at[mine, cols[i]], x_s.at[d - 1, i], x_r.at[d - 1, i], at_x(d))
            for d in (1, 3, 2)
        ]
        for i in range(CHUNKS)
    ]
    onward = [[], [], []]

    def pass_on(n):
        i, s = n // 2, n % 2
        cross[n].wait_recv()
        r = rows(((1 - a) * 4 + x) * FEAT + s * 416, 416, 16)
        for d in (1, 3, 2):
            onward[i].append(
                go(
                    whole.at[r, cols[i]], whole.at[r, cols[i]],
                    f_s.at[d - 1, i, s], f_r.at[d - 1, i, s], at_x(d),
                )
            )

    def states(p, carry):
        r = rows(p * SUB, SUB, SUB)
        for j in range(2):
            sys[p, j] = pack(master[j, r], FIXED / TOP_MASTER)
            sys[p, 2 + j] = pack(first[j, r], FIXED / TOP_FIRST)
            sys[p, 4 + j] = pack(second[j, r], FIXED / TOP_SECOND)
        return carry

    lax.fori_loop(0, 8, states, 0)
    state_y = []
    for d in range(1, 8):
        p = lax.rem(part + d, 8)
        state_y.append(
            go(sys.at[p], syr.at[pl.ds(part * 6, 6)], k_s.at[d - 1], k_r.at[d - 1], at_part(p))
        )
    syr[pl.ds(part * 6, 6)] = sys[part]

    def turn(k, carry):
        wt[k] = w[k].astype(f32).T.astype(jnp.bfloat16)
        return carry

    lax.fori_loop(0, NBLK, turn, 0)
    grad[...] = jnp.zeros_like(grad)
    share = []
    swap = []
    factor = HD ** (-0.5)
    half = rows(c * HROWS, HROWS, 16)
    other = rows((1 - c) * HROWS, HROWS, 16)

    def attend(i):
        if i == 0:
            own.wait()
        for cp in along[i] + onward[i]:
            cp.wait_recv()
        share.append(
            go(whole.at[other, cols[i]], sib.at[:, cols[i]], s_s.at[i], s_r.at[i], sibling)
        )

        def add_q(k, total):
            for m in range(4):
                r = rows((k * 4 + m) * 128, 128, 128)
                total = total + jnp.dot(wt[k * 4 + m], whole[r, cols[i]], preferred_element_type=f32)
            return total

        qt = lax.fori_loop(0, 13, add_q, jnp.zeros((HD, CTOK), f32))
        queries = qt.T.astype(jnp.bfloat16)
        n = (i + 1) * CTOK
        kk = keys[pl.ds(0, n)]
        vv = values[pl.ds(0, n)]
        og = outg[cols[i]]
        scores = dot_t(queries, kk) * factor
        row_pos = lax.broadcasted_iota(jnp.int32, (CTOK, n), 0) + i * CTOK
        col_pos = lax.broadcasted_iota(jnp.int32, (CTOK, n), 1)
        scores = jnp.where(row_pos >= col_pos, scores, -1e30)
        shifted = jnp.exp(scores - jnp.max(scores, axis=1, keepdims=True))
        attention = shifted / jnp.sum(shifted, axis=1, keepdims=True)
        outputs = jnp.dot(attention.astype(jnp.bfloat16), vv, preferred_element_type=f32)
        deltas = jnp.sum(og.astype(f32) * outputs, axis=1, keepdims=True)
        upstream = dot_t(og, vv)
        dscores = (attention * (upstream - deltas)).astype(jnp.bfloat16)
        dquery = jnp.dot(dscores, kk, preferred_element_type=f32) * factor
        dq[0, cols[i]] = dquery.astype(jnp.bfloat16)
        swap.append(go(dq.at[0, cols[i]], dq.at[1, cols[i]], d_s.at[i], d_r.at[i], sibling))

    def add_grad(lo, n):
        tok = pl.ds(lo, n)

        def one(j, top):
            r = rows(j * FEAT, FEAT, 16)
            g = grad[r] + jnp.dot(whole[rows(c * HROWS + j * FEAT, FEAT, 16), tok], dq[0, tok], preferred_element_type=f32)
            g = g + jnp.dot(sib[r, tok], dq[1, tok], preferred_element_type=f32)
            grad[r] = g
            return jnp.maximum(top, jnp.max(jnp.abs(g), axis=0, keepdims=True))

        return lax.fori_loop(0, 4, one, jnp.zeros((1, HD), f32))

    pass_on(0)
    pass_on(1)
    pass_on(2)
    pass_on(3)
    attend(0)
    pass_on(4)
    attend(1)
    pass_on(5)

    for cp in state_y:
        cp.wait_recv()

    def states_z(z, carry):
        for j in range(OWN):
            u = block_code[z * OWN + j] & 63
            for m in range(3):
                szs[z, m * OWN + j] = syr[u + 2 * m]
        return carry

    lax.fori_loop(0, 8, states_z, 0)
    state_z = []
    for d in range(1, 8):
        z = lax.rem(zl + d, 8)
        state_z.append(
            go(szs.at[z], szr.at[pl.ds(zl * 3 * OWN, 3 * OWN)], p_s.at[d - 1], p_r.at[d - 1], at_z(z))
        )
    szr[pl.ds(zl * 3 * OWN, 3 * OWN)] = szs[zl]
    for i in range(2):
        share[i].wait_recv()
        swap[i].wait_recv()
    add_grad(0, 2 * CTOK)
    attend(2)
    share[2].wait_recv()
    swap[2].wait_recv()
    top = add_grad(2 * CTOK, CTOK)

    e = jnp.broadcast_to(level(top), (8, HD))
    inv = inverse_of(e[:1])

    def to_fixed(b, carry):
        for p in range(8):
            ys[p, b] = pack(grad[rows(b * 128 + p * SUB, SUB, SUB)], inv)
        return carry

    lax.fori_loop(0, HALF, to_fixed, 0)
    for p in range(8):
        ys[p, HALF] = e
    to_parts = []
    for d in range(1, 8):
        p = lax.rem(part + d, 8)
        to_parts.append(go(ys.at[p], yr.at[part], y_s.at[d - 1], y_r.at[d - 1], at_part(p)))
    yr[part] = ys[part]
    for cp in to_parts:
        cp.wait_recv()
    steps = [step_of(yr[p, HALF, 0:1]) for p in range(8)]

    def add_y(b, top):
        for h in range(2):
            total = unpack(yr[h, b], steps[h])
            for m in range(1, 4):
                total = total + unpack(yr[2 * m + h, b], steps[2 * m + h])
            gsum[h * HALF + b] = total
            top = jnp.maximum(top, jnp.max(jnp.abs(total), axis=0, keepdims=True))
        return top

    top = lax.fori_loop(0, HALF, add_y, jnp.zeros((1, HD), f32))
    gsum[pl.ds(NBLK, PAD - NBLK)] = jnp.zeros((PAD - NBLK, SUB, HD), f32)

    e = jnp.broadcast_to(level(top), (8, HD))
    inv = inverse_of(e[:1])

    def to_fixed_z(z, carry):
        for j in range(OWN):
            zs[z, j] = pack(gsum[z * OWN + j], inv)
        zs[z, OWN] = e
        return carry

    lax.fori_loop(0, 8, to_fixed_z, 0)
    to_z = []
    for d in range(1, 8):
        z = lax.rem(zl + d, 8)
        to_z.append(go(zs.at[z], zr.at[zl], r_s.at[d - 1], r_r.at[d - 1], at_z(z)))
    zr[zl] = zs[zl]
    for cp in to_z + state_z:
        cp.wait_recv()
    steps = [step_of(zr[z, OWN, 0:1]) for z in range(8)]
    top = jnp.zeros((1, HD), f32)
    part_rows = rows(part * SUB, SUB, SUB)
    for j in range(OWN):
        total = unpack(zr[0, j], steps[0])
        for z in range(1, 8):
            total = total + unpack(zr[z, j], steps[z])
        red[j] = total
        top = jnp.maximum(top, jnp.max(jnp.abs(total), axis=0, keepdims=True))
        u = block_code[zl * OWN + j] >> 6
        m_state = unpack(szr[u + j], TOP_MASTER / FIXED)
        f_state = unpack(szr[u + OWN + j], TOP_FIRST / FIXED)
        s_state = unpack(szr[u + 2 * OWN + j], TOP_SECOND / FIXED)
        nm, _, _ = adam_update(total, m_state, f_state, s_state, 1.0)
        out_w[zl * OWN + j, part_rows] = nm.astype(jnp.bfloat16)

    def weights(z, r):
        return out_w.at[pl.ds(z * OWN, OWN), r]

    w_z = []
    for d in range(1, 8):
        z = lax.rem(zl + d, 8)
        w_z.append(go(weights(zl, part_rows), weights(zl, part_rows), w_s.at[d - 1], w_r.at[d - 1], at_z(z)))
    e = jnp.broadcast_to(level(top), (8, HD))
    inv = inverse_of(e[:1])
    for j in range(OWN):
        gq[zl * 8 + j] = pack(red[j], inv)
    gq[zl * 8 + OWN] = e
    g_z = []
    for d in range(1, 8):
        z = lax.rem(zl + d, 8)
        at = gq.at[pl.ds(zl * 8, 8)]
        g_z.append(go(at, at, a_s.at[d - 1], a_r.at[d - 1], at_z(z)))

    to_y = []
    to_core = []
    for d in range(8):
        z = lax.rem(zl - d + 8, 8)
        if d:
            w_z[d - 1].wait_recv()
        at = weights(z, part_rows)
        to_y.append(
            [
                go(at, at, v_s.at[q - 1, d], v_r.at[q - 1, d], at_part(lax.rem(y + q, 4) * 2 + c))
                for q in (1, 3, 2)
            ]
        )
        to_core.append(go(at, at, c_s.at[0, d], c_r.at[0, d], sibling))

    for cp in g_z:
        cp.wait_recv()
    for p in range(8):
        for j in range(2):
            u = slot_code[zl * 16 + p * 2 + j] & 63
            send_g[p, j] = unpack(gq[u], step_of(gq[u | OWN][:1]))
    to_owner = []
    for d in range(1, 8):
        p = lax.rem(part + d, 8)
        to_owner.append(go(send_g.at[p], recv_g.at[part], o_s.at[d - 1], o_r.at[d - 1], at_part(p)))
    recv_g[part] = send_g[part]
    for d in range(8):
        z = lax.rem(zl - d + 8, 8)
        for n, q in enumerate((1, 3, 2)):
            to_y[d][n].wait_recv()
            r = rows((lax.rem(y - q + 4, 4) * 2 + c) * SUB, SUB, SUB)
            at = weights(z, r)
            to_core.append(go(at, at, c_s.at[q, d], c_r.at[q, d], sibling))
    for cp in to_owner:
        cp.wait_recv()
    for j in range(2):
        used = (slot_code[dp * 2 + j] >> 6).astype(f32)
        for p in range(8):
            r = pl.ds(p * SUB, SUB)
            nm, nf, ns = adam_update(recv_g[p, j], master[j, r], first[j, r], second[j, r], used)
            out_m[j, r] = nm
            out_f[j, r] = nf
            out_s[j, r] = ns
    for cp in to_core:
        cp.wait_recv()
    for cp in sent:
        cp.wait_send()


def body(
    activation, w_query, key_rows, value_rows, out_grad, owners, master_copy, first_moment, second_moment
):
    own_row = owners[0, :, 0]
    order = jnp.arange(NBLK, dtype=jnp.int32)
    earlier = (own_row[:, None] == own_row[None, :]) & (order[:, None] < order[None, :])
    second_slot = jnp.sum(earlier.astype(jnp.int32), axis=0)
    target = own_row * 2 + second_slot
    match = target[None, :] == jnp.arange(128, dtype=jnp.int32)[:, None]
    place = 64 + (order // OWN) * 8 + order % OWN
    slot_code = jnp.sum(jnp.where(match, place[None, :], 0), axis=1)
    block_code = (own_row // 8) * (3 * OWN * 64) + (own_row % 8) * 6 + second_slot
    block_code = jnp.pad(block_code, (0, PAD - NBLK))
    smem = pl.BlockSpec(memory_space=pltpu.SMEM)
    vmem = pl.BlockSpec(memory_space=pltpu.VMEM)
    f32 = jnp.float32
    bf16 = jnp.bfloat16
    i32 = jnp.int32
    dma = pltpu.SemaphoreType.DMA

    def pair(*dims):
        return [dma(dims), dma(dims)]

    new_w, new_m, new_f, new_s = pl.pallas_call(
        kernel,
        out_shape=(
            jax.ShapeDtypeStruct((PAD, 128, HD), bf16),
            jax.ShapeDtypeStruct((2, 128, HD), f32),
            jax.ShapeDtypeStruct((2, 128, HD), f32),
            jax.ShapeDtypeStruct((2, 128, HD), f32),
        ),
        in_specs=[smem] * 2 + [vmem] * 8,
        out_specs=(vmem,) * 4,
        scratch_shapes=[
            pltpu.VMEM((8 * FEAT, TOK), bf16),
            pltpu.VMEM((HROWS, TOK), bf16),
            pltpu.VMEM((NBLK, HD, 128), bf16),
            pltpu.VMEM((2, TOK, HD), bf16),
            pltpu.VMEM((HROWS, HD), f32),
            pltpu.VMEM((8, HALF + 1, 8, HD), i32),
            pltpu.VMEM((8, HALF + 1, 8, HD), i32),
            pltpu.VMEM((PAD, SUB, HD), f32),
            pltpu.VMEM((8, OWN + 1, 8, HD), i32),
            pltpu.VMEM((8, OWN + 1, 8, HD), i32),
            pltpu.VMEM((OWN, SUB, HD), f32),
            pltpu.VMEM((64, 8, HD), i32),
            pltpu.VMEM((8, 6, 8, HD), i32),
            pltpu.VMEM((48, 8, HD), i32),
            pltpu.VMEM((8, 3 * OWN, 8, HD), i32),
            pltpu.VMEM((8 * 3 * OWN, 8, HD), i32),
            pltpu.VMEM((8, 2, SUB, HD), f32),
            pltpu.VMEM((8, 2, SUB, HD), f32),
        ]
        + pair(CHUNKS, 2)
        + pair(3, CHUNKS)
        + pair(3, CHUNKS, 2)
        + pair(CHUNKS)
        + pair(CHUNKS)
        + pair(7)
        + pair(7)
        + pair(7)
        + pair(7)
        + pair(7)
        + pair(3, 8)
        + pair(4, 8)
        + pair(7)
        + pair(7)
        + [dma],
        compiler_params=pltpu.CompilerParams(
            collective_id=0, has_side_effects=True, vmem_limit_bytes=56 * 2**20
        ),
        name="project_back",
    )(
        slot_code, block_code,
        activation.T, w_query.reshape(NBLK, 128, HD), key_rows, value_rows, out_grad,
        master_copy, first_moment, second_moment,
    )
    return (new_w.reshape(PAD * 128, HD)[: NBLK * 128], new_m, new_f, new_s)


def solution(mesh):
    return jax.shard_map(
        body,
        mesh=mesh,
        in_specs=(
            P("dp", "tensor"),
            P(None, "tensor"),
            P("dp", "tensor"),
            P("dp", "tensor"),
            P("dp", "tensor"),
            P("tensor", None, None),
            P("dp", None, "tensor"),
            P("dp", None, "tensor"),
            P("dp", None, "tensor"),
        ),
        out_specs=(
            P(None, "tensor"),
            P("dp", None, "tensor"),
            P("dp", None, "tensor"),
            P("dp", None, "tensor"),
        ),
        check_vma=False,
    )
```

```python
import functools

import jax
import jax.numpy as jnp
from jax import lax
from jax.experimental import pallas as pl
from jax.experimental.pallas import tpu as pltpu
from jax.sharding import PartitionSpec as P

beta_first = 0.9
beta_second = 0.95
learn_rate = 0.001
adam_eps = 1e-08
adam_step = 100.0

MESH = pl.DeviceIdType.MESH
TOK = 384
FEAT = 832
HD = 128
NBLK = 52
HALF = 26
HROWS = HALF * 128
SUB = 16
OWN = 7
PAD = 8 * OWN
CHUNKS = 3
CTOK = TOK // CHUNKS
LEVELS = 32700.0
FIXED = 32766.0
TOP_MASTER = 0.078125
TOP_FIRST = 4.0
TOP_SECOND = 1.0


def adam_update(gradient, master, first, second, used):
    first_new = beta_first * first + (1.0 - beta_first) * gradient
    second_new = beta_second * second + (1.0 - beta_second) * gradient * gradient
    corr_first = 1.0 - beta_first**adam_step
    corr_second = 1.0 - beta_second**adam_step
    master_new = master - learn_rate * (first_new / corr_first) / (
        jnp.sqrt(second_new / corr_second) + adam_eps
    )
    return (master_new * used, first_new * used, second_new * used)


def dot_t(a, b):
    return lax.dot_general(a, b, (((1,), (1,)), ((), ())), preferred_element_type=jnp.float32)


def dot_0(a, b):
    return lax.dot_general(a, b, (((0,), (0,)), ((), ())), preferred_element_type=jnp.float32)


def pack(v, inv):
    q = jnp.round(v * inv).astype(jnp.int32)
    return (q[:8] << 16) | (q[8:] & 0xFFFF)


def unpack(u, step):
    return jnp.concatenate([u >> 16, (u << 16) >> 16], axis=0).astype(jnp.float32) * step


def level(top):
    bits = jnp.log(jnp.maximum(top, 1e-30)) * (8.0 / 0.6931471805599453)
    return jnp.ceil(bits).astype(jnp.int32)


def step_of(e):
    return jnp.exp(e.astype(jnp.float32) * (0.6931471805599453 / 8.0)) * (1.0 / LEVELS)


def inverse_of(e):
    return jnp.exp(e.astype(jnp.float32) * (-0.6931471805599453 / 8.0)) * LEVELS


def kernel(
    slot_code, block_code,
    act, w, keys, values, outg, master, first, second,
    out_w, out_m, out_f, out_s,
    whole, sib, wt, wo, qo, po, pr, dqs, dqa, grad, ys, yr, gsum, zs, zr, red, gq,
    sys, syr, szs, szr, wst, send_g, recv_g,
    x_s, x_r, s_s, s_r, b_s, b_r, q_s, q_r, h_s, h_r, d_s, d_r, y_s, y_r, r_s, r_r,
    a_s, a_r, o_s, o_r, w_s, w_r, v_s, v_r, c_s, c_r, k_s, k_r, p_s, p_r, l_sem,
):
    dp = lax.axis_index("dp")
    t = lax.axis_index("tensor")
    zl = dp // 8
    part = lax.rem(dp, 8)
    y = part // 2
    c = lax.rem(part, 2)
    a = t // 4
    x = lax.rem(t, 4)
    f32 = jnp.float32
    bf16 = jnp.bfloat16

    def device(z, y, c, a):
        return (z * 8 + y * 2 + c, a * 4 + x)

    def at_x(d):
        return (dp, a * 4 + lax.rem(x + d, 4))

    def at_part(p):
        return (zl * 8 + p, t)

    def at_z(z):
        return (z * 8 + part, t)

    opposite = device(zl, y, c, 1 - a)
    sibling = device(zl, y, 1 - c, a)

    def rows(start, n, unit):
        return pl.ds(pl.multiple_of(start, unit), n)

    barrier = pltpu.get_barrier_semaphore()
    peers = [at_x(d) for d in (1, 2, 3)] + [opposite]
    peers += [at_part(lax.rem(part + d, 8)) for d in range(1, 8)]
    peers += [at_z(lax.rem(zl + d, 8)) for d in range(1, 8)]
    peers += [device(lax.rem(zl + d, 8), y, 1 - c, 1 - a) for d in range(8)]
    for peer in peers:
        pl.semaphore_signal(barrier, inc=1, device_id=peer, device_id_type=MESH)

    def turn(k, carry):
        wt[rows(k * 128, 128, 128)] = w[k].astype(f32).T.astype(bf16)
        return carry

    lax.fori_loop((1 - a) * HALF, (1 - a) * HALF + HALF, turn, 0)
    pl.semaphore_wait(barrier, len(peers))
    sent = []

    def copy(src, dst, ss, rs, dev):
        return pltpu.make_async_remote_copy(
            src_ref=src, dst_ref=dst, send_sem=ss, recv_sem=rs, device_id=dev, device_id_type=MESH
        )

    def go(src, dst, ss, rs, dev):
        cp = copy(src, dst, ss, rs, dev)
        cp.start()
        sent.append(cp)
        return cp

    eighth = rows(part * 416, 416, 16)
    w_cross = go(
        wt.at[rows((1 - a) * HROWS + part * 416, 416, 16)], wo.at[eighth],
        b_s.at[0], b_r.at[0], opposite,
    )

    cols = [pl.ds(i * CTOK, CTOK) for i in range(CHUNKS)]
    mine = rows(x * FEAT, FEAT, 16)
    own = pltpu.make_async_copy(act, whole.at[mine], l_sem)
    own.start()
    along = [
        [
            go(act.at[:, cols[i]], whole.at[mine, cols[i]], x_s.at[d - 1, i], x_r.at[d - 1, i], at_x(d))
            for d in (1, 3, 2)
        ]
        for i in range(CHUNKS)
    ]

    def states(p, carry):
        for j in range(2):
            for s in range(2):
                r = rows((p // 2) * 32 + s * SUB, SUB, SUB)
                n = j * 2 + s
                sys[p, n] = pack(master[j, r], FIXED / TOP_MASTER)
                sys[p, 4 + n] = pack(first[j, r], FIXED / TOP_FIRST)
                sys[p, 8 + n] = pack(second[j, r], FIXED / TOP_SECOND)
        return carry

    lax.fori_loop(0, 8, states, 0)
    state_y = []
    for d in range(1, 8):
        p = lax.rem(part + d, 8)
        state_y.append(
            go(sys.at[p], syr.at[pl.ds(part * 12, 12)], k_s.at[d - 1], k_r.at[d - 1], at_part(p))
        )
    syr[pl.ds(part * 12, 12)] = sys[part]
    lax.fori_loop(a * HALF, a * HALF + HALF, turn, 0)
    for cp in state_y:
        cp.wait_recv()

    def states_z(z, carry):
        for j in range(OWN):
            u = z * OWN + j
            at = (block_code[c * HALF + u // 2] & 127) + lax.rem(u, 2)
            for m in range(3):
                szs[m, z, j] = syr[at + 4 * m]
        return carry

    lax.fori_loop(0, 8, states_z, 0)
    state_z = []

    def send_states(m):
        szr[m, pl.ds(zl * OWN, OWN)] = szs[m, zl]
        for d in range(1, 8):
            z = lax.rem(zl + d, 8)
            state_z.append(
                go(
                    szs.at[m, z], szr.at[m, pl.ds(zl * OWN, OWN)],
                    p_s.at[m, d - 1], p_r.at[m, d - 1], at_z(z),
                )
            )

    send_states(0)
    send_states(1)
    w_cross.wait_recv()
    w_part = []
    for d in range(1, 8):
        p = lax.rem(part + d, 8)
        w_part.append(go(wo.at[eighth], wo.at[eighth], b_s.at[d], b_r.at[d], at_part(p)))

    def partial(weights, first_row, i):
        def add_q(k, total):
            for m in range(13):
                n = k * 13 + m
                total = total + jnp.dot(
                    weights[rows(first_row + n * 128, 128, 128)],
                    whole[rows(n * 128, 128, 128), cols[i]],
                    preferred_element_type=f32,
                )
            return total

        return lax.fori_loop(0, 2, add_q, jnp.zeros((HD, CTOK), f32))

    own.wait()
    share = []
    for i in range(CHUNKS):
        for cp in along[i]:
            cp.wait_recv()
        share.append(go(whole.at[:, cols[i]], sib.at[:, cols[i]], s_s.at[i], s_r.at[i], sibling))
        qo[i] = partial(wt, a * HROWS, i)
    for cp in w_part:
        cp.wait_recv()
    q_cross = []
    for i in range(CHUNKS):
        po[i] = partial(wo, 0, i)
        q_cross.append(go(po.at[i], pr.at[i], q_s.at[i], q_r.at[i], opposite))

    factor = HD ** (-0.5)
    same = a == c
    dq_cross = []
    for i in range(CHUNKS):
        q_cross[i].wait_recv()
        queries = (qo[i] + pr[i]).T.astype(bf16)
        n = (i + 1) * CTOK
        kk = keys[pl.ds(0, n)]
        vv = values[pl.ds(0, n)]
        og = outg[cols[i]]
        scores = dot_t(queries, kk) * factor
        row_pos = lax.broadcasted_iota(jnp.int32, (CTOK, n), 0) + i * CTOK
        col_pos = lax.broadcasted_iota(jnp.int32, (CTOK, n), 1)
        scores = jnp.where(row_pos >= col_pos, scores, -1e30)
        shifted = jnp.exp(scores - jnp.max(scores, axis=1, keepdims=True))
        attention = shifted / jnp.sum(shifted, axis=1, keepdims=True)
        outputs = jnp.dot(attention.astype(bf16), vv, preferred_element_type=f32)
        deltas = jnp.sum(og.astype(f32) * outputs, axis=1, keepdims=True)
        upstream = dot_t(og, vv)
        dscores = (attention * (upstream - deltas)).astype(bf16)
        dquery = jnp.dot(dscores, kk, preferred_element_type=f32) * factor
        dqs[cols[i]] = dquery.astype(bf16)
        go(
            dqs.at[cols[i]], dqa.at[c, cols[i]], d_s.at[i], d_r.at[i, c], device(zl, y, a, 1 - a)
        )

        @pl.when(same)
        def _():
            dqa[c, cols[i]] = dqs[cols[i]]

        @pl.when(jnp.logical_not(same))
        def _():
            copy(dqs.at[cols[i]], dqa.at[c, cols[i]], h_s.at[i], h_r.at[i], sibling).start()

    send_states(2)

    def wait_dq(i):
        @pl.when(same)
        def _():
            copy(dqs.at[cols[i]], dqa.at[1 - c, cols[i]], h_s.at[i], h_r.at[i], sibling).wait_recv()

        @pl.when(jnp.logical_not(same))
        def _():
            for s in range(2):
                copy(
                    dqs.at[cols[i]], dqa.at[s, cols[i]], d_s.at[i], d_r.at[i, s], opposite
                ).wait_recv()
            copy(dqs.at[cols[i]], dqa.at[c, cols[i]], h_s.at[i], h_r.at[i], sibling).wait_send()

    def add_grad(lo, n, fresh):
        tok = pl.ds(lo, n)

        def one(j, top):
            r = rows(j * FEAT, FEAT, 16)
            g = jnp.dot(whole[r, tok], dqa[c, tok], preferred_element_type=f32)
            g = g + jnp.dot(sib[r, tok], dqa[1 - c, tok], preferred_element_type=f32)
            if not fresh:
                g = g + grad[r]
            grad[r] = g
            return jnp.maximum(top, jnp.max(jnp.abs(g), axis=0, keepdims=True))

        return lax.fori_loop(0, 4, one, jnp.zeros((1, HD), f32))

    for cp in share:
        cp.wait_recv()
    wait_dq(0)
    wait_dq(1)
    add_grad(0, 2 * CTOK, True)
    wait_dq(2)
    top = add_grad(2 * CTOK, CTOK, False)

    e = jnp.broadcast_to(level(top), (8, HD))
    inv = inverse_of(e[:1])

    def to_fixed(b, carry):
        for p in range(4):
            for s in range(2):
                ys[p, b * 2 + s] = pack(grad[rows(b * 128 + p * 32 + s * SUB, SUB, SUB)], inv)
        return carry

    lax.fori_loop(0, HALF, to_fixed, 0)
    for p in range(4):
        ys[p, NBLK] = e
    to_y = []
    for d in (1, 3, 2):
        p = lax.rem(y + d, 4)
        to_y.append(go(ys.at[p], yr.at[y], y_s.at[d - 1], y_r.at[d - 1], device(zl, p, c, a)))
    yr[y] = ys[y]
    for cp in to_y:
        cp.wait_recv()
    steps = [step_of(yr[p, NBLK, 0:1]) for p in range(4)]

    def add_y(b, top):
        for s in range(2):
            u = b * 2 + s
            total = unpack(yr[0, u], steps[0])
            for p in range(1, 4):
                total = total + unpack(yr[p, u], steps[p])
            gsum[u] = total
            top = jnp.maximum(top, jnp.max(jnp.abs(total), axis=0, keepdims=True))
        return top

    top = lax.fori_loop(0, HALF, add_y, jnp.zeros((1, HD), f32))
    gsum[pl.ds(NBLK, PAD - NBLK)] = jnp.zeros((PAD - NBLK, SUB, HD), f32)

    e = jnp.broadcast_to(level(top), (8, HD))
    inv = inverse_of(e[:1])

    def to_fixed_z(z, carry):
        for j in range(OWN):
            zs[z, j] = pack(gsum[z * OWN + j], inv)
        zs[z, OWN] = e
        return carry

    lax.fori_loop(0, 8, to_fixed_z, 0)
    to_z = []
    for d in range(1, 8):
        z = lax.rem(zl + d, 8)
        to_z.append(go(zs.at[z], zr.at[zl], r_s.at[d], r_r.at[d], device(z, y, a, c)))
    turned = copy(zs.at[zl], zr.at[zl], r_s.at[0], r_r.at[0], device(zl, y, 1 - c, 1 - a))

    @pl.when(same)
    def _():
        zr[zl] = zs[zl]

    @pl.when(jnp.logical_not(same))
    def _():
        turned.start()
        turned.wait()

    for cp in to_z + state_z:
        cp.wait_recv()
    steps = [step_of(zr[z, OWN, 0:1]) for z in range(8)]
    top = jnp.zeros((1, HD), f32)
    for j in range(OWN):
        total = unpack(zr[0, j], steps[0])
        for z in range(1, 8):
            total = total + unpack(zr[z, j], steps[z])
        red[j] = total
        top = jnp.maximum(top, jnp.max(jnp.abs(total), axis=0, keepdims=True))
        u = zl * OWN + j
        at = (block_code[c * HALF + u // 2] >> 7) + j
        m_state = unpack(szr[0, at], TOP_MASTER / FIXED)
        f_state = unpack(szr[1, at], TOP_FIRST / FIXED)
        s_state = unpack(szr[2, at], TOP_SECOND / FIXED)
        nm, _, _ = adam_update(total, m_state, f_state, s_state, 1.0)
        wst[part, u] = nm.astype(bf16)

    def weights(z, p):
        return wst.at[p, pl.ds(z * OWN, OWN)]

    w_z = []
    for d in range(1, 8):
        z = lax.rem(zl + d, 8)
        w_z.append(go(weights(zl, part), weights(zl, part), w_s.at[d - 1], w_r.at[d - 1], at_z(z)))
    e = jnp.broadcast_to(level(top), (8, HD))
    inv = inverse_of(e[:1])
    for j in range(OWN):
        gq[zl * 8 + j] = pack(red[j], inv)
    gq[zl * 8 + OWN] = e
    g_z = []
    for d in range(1, 8):
        z = lax.rem(zl + d, 8)
        at = gq.at[pl.ds(zl * 8, 8)]
        g_z.append(go(at, at, a_s.at[d - 1], a_r.at[d - 1], at_z(z)))

    back_y = []
    to_core = []
    for d in range(8):
        z = lax.rem(zl - d + 8, 8)
        if d:
            w_z[d - 1].wait_recv()
        at = weights(z, part)
        back_y.append(
            [
                go(at, at, v_s.at[q - 1, d], v_r.at[q - 1, d], device(zl, lax.rem(y + q, 4), c, a))
                for q in (1, 3, 2)
            ]
        )
        to_core.append(go(at, at, c_s.at[0, d], c_r.at[0, d], sibling))

    for cp in g_z:
        cp.wait_recv()
    for p in range(8):
        for j in range(2):
            code = slot_code[zl * 16 + p * 2 + j]
            for s in range(2):
                u = (code >> (6 * s)) & 63
                send_g[p, j * 2 + s] = unpack(gq[u], step_of(gq[u | OWN][:1]))
    to_owner = []
    for d in range(1, 8):
        p = lax.rem(part + d, 8)
        to_owner.append(
            go(send_g.at[p], recv_g.at[pl.ds(part * 4, 4)], o_s.at[d - 1], o_r.at[d - 1], at_part(p))
        )
    recv_g[pl.ds(part * 4, 4)] = send_g[part]
    for d in range(8):
        z = lax.rem(zl - d + 8, 8)
        for n, q in enumerate((1, 3, 2)):
            back_y[d][n].wait_recv()
            at = weights(z, lax.rem(y - q + 4, 4) * 2 + c)
            to_core.append(go(at, at, c_s.at[q, d], c_r.at[q, d], sibling))
    for cp in to_owner:
        cp.wait_recv()
    for j in range(2):
        code = slot_code[dp * 2 + j]
        used = (code >> 13).astype(f32)
        h = ((code >> 12) & 1) * 4
        for n in range(4):
            for s in range(2):
                g = recv_g[h + (n * 8 + j * 2 + s)]
                r = pl.ds(n * 32 + s * SUB, SUB)
                nm, nf, ns = adam_update(g, master[j, r], first[j, r], second[j, r], used)
                out_m[j, r] = nm
                out_f[j, r] = nf
                out_s[j, r] = ns
    for cp in to_core:
        cp.wait_recv()

    def place(b, carry):
        for p in range(8):
            for s in range(2):
                out_w[(p % 2) * HALF + b, (p // 2) * 32 + s * SUB : (p // 2) * 32 + (s + 1) * SUB] = wst[p, b * 2 + s]
        return carry

    lax.fori_loop(0, HALF, place, 0)
    for cp in sent:
        cp.wait_send()


def body(
    activation, w_query, key_rows, value_rows, out_grad, owners, master_copy, first_moment, second_moment
):
    own_row = owners[0, :, 0]
    order = jnp.arange(NBLK, dtype=jnp.int32)
    earlier = (own_row[:, None] == own_row[None, :]) & (order[:, None] < order[None, :])
    second_slot = jnp.sum(earlier.astype(jnp.int32), axis=0)
    target = own_row * 2 + second_slot
    match = target[None, :] == jnp.arange(128, dtype=jnp.int32)[:, None]
    unit = (order % HALF) * 2
    place = (unit // OWN) * 8 + unit % OWN
    place = place + 64 * (((unit + 1) // OWN) * 8 + (unit + 1) % OWN)
    place = place + 4096 * (order // HALF) + 8192
    slot_code = jnp.sum(jnp.where(match, place[None, :], 0), axis=1)
    block_code = (own_row // 8) * (OWN * 128) + (own_row % 8) * 12 + second_slot * 2
    block_code = jnp.pad(block_code, (0, PAD - NBLK))
    smem = pl.BlockSpec(memory_space=pltpu.SMEM)
    vmem = pl.BlockSpec(memory_space=pltpu.VMEM)
    f32 = jnp.float32
    bf16 = jnp.bfloat16
    i32 = jnp.int32
    dma = pltpu.SemaphoreType.DMA

    def pair(*dims):
        return [dma(dims), dma(dims)]

    new_w, new_m, new_f, new_s = pl.pallas_call(
        kernel,
        out_shape=(
            jax.ShapeDtypeStruct((NBLK, 128, HD), bf16),
            jax.ShapeDtypeStruct((2, 128, HD), f32),
            jax.ShapeDtypeStruct((2, 128, HD), f32),
            jax.ShapeDtypeStruct((2, 128, HD), f32),
        ),
        in_specs=[smem] * 2 + [vmem] * 8,
        out_specs=(vmem,) * 4,
        scratch_shapes=[
            pltpu.VMEM((HROWS, TOK), bf16),
            pltpu.VMEM((HROWS, TOK), bf16),
            pltpu.VMEM((2 * HROWS, 128), bf16),
            pltpu.VMEM((HROWS, 128), bf16),
            pltpu.VMEM((CHUNKS, HD, CTOK), f32),
            pltpu.VMEM((CHUNKS, HD, CTOK), f32),
            pltpu.VMEM((CHUNKS, HD, CTOK), f32),
            pltpu.VMEM((TOK, HD), bf16),
            pltpu.VMEM((2, TOK, HD), bf16),
            pltpu.VMEM((HROWS, HD), f32),
            pltpu.VMEM((4, NBLK + 1, 8, HD), i32),
            pltpu.VMEM((4, NBLK + 1, 8, HD), i32),
            pltpu.VMEM((PAD, SUB, HD), f32),
            pltpu.VMEM((8, OWN + 1, 8, HD), i32),
            pltpu.VMEM((8, OWN + 1, 8, HD), i32),
            pltpu.VMEM((OWN, SUB, HD), f32),
            pltpu.VMEM((64, 8, HD), i32),
            pltpu.VMEM((8, 12, 8, HD), i32),
            pltpu.VMEM((96, 8, HD), i32),
            pltpu.VMEM((3, 8, OWN, 8, HD), i32),
            pltpu.VMEM((3, PAD, 8, HD), i32),
            pltpu.VMEM((8, PAD, SUB, HD), bf16),
            pltpu.VMEM((8, 4, SUB, HD), f32),
            pltpu.VMEM((32, SUB, HD), f32),
        ]
        + pair(3, CHUNKS)
        + pair(CHUNKS)
        + pair(8)
        + pair(CHUNKS)
        + pair(CHUNKS)
        + [dma((CHUNKS,)), dma((CHUNKS, 2))]
        + pair(3)
        + pair(8)
        + pair(7)
        + pair(7)
        + pair(7)
        + pair(3, 8)
        + pair(4, 8)
        + pair(7)
        + pair(3, 7)
        + [dma],
        compiler_params=pltpu.CompilerParams(
            collective_id=0, has_side_effects=True, vmem_limit_bytes=56 * 2**20
        ),
        name="project_back",
    )(
        slot_code, block_code,
        activation.T, w_query.reshape(NBLK, 128, HD), key_rows, value_rows, out_grad,
        master_copy, first_moment, second_moment,
    )
    return (new_w.reshape(NBLK * 128, HD), new_m, new_f, new_s)


def solution(mesh):
    return jax.shard_map(
        body,
        mesh=mesh,
        in_specs=(
            P("dp", "tensor"),
            P(None, "tensor"),
            P("dp", "tensor"),
            P("dp", "tensor"),
            P("dp", "tensor"),
            P("tensor", None, None),
            P("dp", None, "tensor"),
            P("dp", None, "tensor"),
            P("dp", None, "tensor"),
        ),
        out_specs=(
            P(None, "tensor"),
            P("dp", None, "tensor"),
            P("dp", None, "tensor"),
            P("dp", None, "tensor"),
        ),
        check_vma=False,
    )
```

```python
import functools

import jax
import jax.numpy as jnp
from jax import lax
from jax.experimental import pallas as pl
from jax.experimental.pallas import tpu as pltpu
from jax.sharding import PartitionSpec as P

beta_first = 0.9
beta_second = 0.95
learn_rate = 0.001
adam_eps = 1e-08
adam_step = 100.0

MESH = pl.DeviceIdType.MESH
TOK = 384
FEAT = 832
HD = 128
NBLK = 52
HALF = 26
HROWS = HALF * 128
SUB = 16
OWN = 7
PAD = 8 * OWN
CHUNKS = 3
CTOK = TOK // CHUNKS
LEVELS = 32700.0
FINE = 8388000.0
FIXED = 32766.0
TOP_MASTER = 0.078125
TOP_FIRST = 4.0
TOP_SECOND = 1.0


def adam_update(gradient, master, first, second, used):
    first_new = beta_first * first + (1.0 - beta_first) * gradient
    second_new = beta_second * second + (1.0 - beta_second) * gradient * gradient
    corr_first = 1.0 - beta_first**adam_step
    corr_second = 1.0 - beta_second**adam_step
    master_new = master - learn_rate * (first_new / corr_first) / (
        jnp.sqrt(second_new / corr_second) + adam_eps
    )
    return (master_new * used, first_new * used, second_new * used)


def dot_t(a, b):
    return lax.dot_general(a, b, (((1,), (1,)), ((), ())), preferred_element_type=jnp.float32)


def dot_0(a, b):
    return lax.dot_general(a, b, (((0,), (0,)), ((), ())), preferred_element_type=jnp.float32)


def pack(v, inv):
    q = jnp.round(v * inv).astype(jnp.int32)
    k = q.shape[0] // 2
    return (q[:k] << 16) | (q[k:] & 0xFFFF)


def unpack(u, step):
    return jnp.concatenate([u >> 16, (u << 16) >> 16], axis=0).astype(jnp.float32) * step


def pack_fine(v, inv):
    q = jnp.round(v * inv).astype(jnp.int32)
    last = q[96:]
    return jnp.concatenate(
        [
            (q[0:32] << 8) | (last & 255),
            (q[32:64] << 8) | ((last >> 8) & 255),
            (q[64:96] << 8) | ((last >> 16) & 255),
        ],
        axis=0,
    )


def unpack_fine(u, step):
    last = ((u[64:96] << 24) >> 8) | ((u[32:64] & 255) << 8) | (u[0:32] & 255)
    return jnp.concatenate([u >> 8, last], axis=0).astype(jnp.float32) * step


def level(top):
    bits = jnp.log(jnp.maximum(top, 1e-30)) * (8.0 / 0.6931471805599453)
    return jnp.ceil(bits).astype(jnp.int32)


def step_of(e):
    return jnp.exp(e.astype(jnp.float32) * (0.6931471805599453 / 8.0)) * (1.0 / LEVELS)


def inverse_of(e):
    return jnp.exp(e.astype(jnp.float32) * (-0.6931471805599453 / 8.0)) * LEVELS


def kernel(
    slot_code, block_code,
    act, w, keys, values, outg, master, first, second,
    wst, recv_g,
    whole, sib, wt, wo, qo, po, pr, pm, pn, dqs, dqa, grad, ys, yr, gsum, zs, zr, red, gq,
    sys, syr, szs, szr, send_g,
    x_s, x_r, f_s, f_r, s_s, s_r, b_s, b_r, q_s, q_r, n_s, n_r, h_s, h_r, d_s, d_r, y_s, y_r, r_s, r_r,
    a_s, a_r, o_s, o_r, w_s, w_r, v_s, v_r, c_s, c_r, k_s, k_r, p_s, p_r, l_sem,
):
    dp = lax.axis_index("dp")
    t = lax.axis_index("tensor")
    zl = dp // 8
    part = lax.rem(dp, 8)
    y = part // 2
    c = lax.rem(part, 2)
    a = t // 4
    x = lax.rem(t, 4)
    f32 = jnp.float32
    bf16 = jnp.bfloat16

    def device(z, y, c, a):
        return (z * 8 + y * 2 + c, a * 4 + x)

    def at_x(d):
        return (dp, a * 4 + lax.rem(x + d, 4))

    def at_part(p):
        return (zl * 8 + p, t)

    def at_z(z):
        return (z * 8 + part, t)

    opposite = device(zl, y, c, 1 - a)
    sibling = device(zl, y, 1 - c, a)

    def rows(start, n, unit):
        return pl.ds(pl.multiple_of(start, unit), n)

    barrier = pltpu.get_barrier_semaphore()
    peers = [at_x(d) for d in (1, 2, 3)] + [opposite]
    peers += [at_part(lax.rem(part + d, 8)) for d in range(1, 8)]
    peers += [at_z(lax.rem(zl + d, 8)) for d in range(1, 8)]
    peers += [device(lax.rem(zl + d, 8), y, 1 - c, 1 - a) for d in range(8)]
    for peer in peers:
        pl.semaphore_signal(barrier, inc=1, device_id=peer, device_id_type=MESH)

    def turn(k, carry):
        r = rows(k * 128, 128, 128)
        wt[r, 0:128] = w[k * 2].astype(f32).T.astype(bf16)
        wt[r, 128:256] = w[k * 2 + 1].astype(f32).T.astype(bf16)
        return carry

    lax.fori_loop(0, HALF, turn, 0)

    def states(p, carry):
        for j in range(2):
            for s in range(2):
                r = rows((p // 2) * 32 + s * SUB, SUB, SUB)
                n = j * 2 + s
                sys[p, n] = pack(master[j, r], FIXED / TOP_MASTER)
                sys[p, 4 + n] = pack(first[j, r], FIXED / TOP_FIRST)
                sys[p, 8 + n] = pack(second[j, r], FIXED / TOP_SECOND)
        return carry

    lax.fori_loop(0, 8, states, 0)
    pl.semaphore_wait(barrier, len(peers))
    sent = []

    def copy(src, dst, ss, rs, dev):
        return pltpu.make_async_remote_copy(
            src_ref=src, dst_ref=dst, send_sem=ss, recv_sem=rs, device_id=dev, device_id_type=MESH
        )

    def go(src, dst, ss, rs, dev):
        cp = copy(src, dst, ss, rs, dev)
        cp.start()
        sent.append(cp)
        return cp

    eighth = rows(part * 208, 208, 16)
    w_cross = go(
        wt.at[rows((1 - a) * (HROWS // 2) + part * 208, 208, 16)], wo.at[eighth],
        b_s.at[0], b_r.at[0], opposite,
    )

    cols = [pl.ds(i * CTOK, CTOK) for i in range(CHUNKS)]
    mine = rows(x * FEAT, FEAT, 16)
    own = pltpu.make_async_copy(act, whole.at[mine], l_sem)
    own.start()
    order = (2, 1, 0)
    along = {
        i: [
            go(act.at[:, cols[i]], whole.at[mine, cols[i]], x_s.at[n, i], x_r.at[n, i], at_x(d))
            for n, d in enumerate((1, 3))
        ]
        for i in order
    }
    onward = {}

    def pass_on(i):
        onward[i] = []
        for n, d in enumerate((1, 3)):
            along[i][n].wait_recv()
            r = rows(lax.rem(x - d + 4, 4) * FEAT + n * 416, 416, 16)
            at = whole.at[r, cols[i]]
            onward[i].append(go(at, at, f_s.at[n, i], f_r.at[n, i], at_x(d)))

    state_y = []
    for d in range(1, 8):
        p = lax.rem(part + d, 8)
        state_y.append(
            go(sys.at[p], syr.at[pl.ds(part * 12, 12)], k_s.at[d - 1], k_r.at[d - 1], at_part(p))
        )
    syr[pl.ds(part * 12, 12)] = sys[part]
    for cp in state_y:
        cp.wait_recv()

    def states_z(z, carry):
        for j in range(OWN):
            u = z * OWN + j
            at = (block_code[jnp.minimum(c * HALF + u // 2, NBLK - 1)] & 127) + lax.rem(u, 2)
            for m in range(3):
                szs[m, z, j] = syr[at + 4 * m]
        return carry

    lax.fori_loop(0, 8, states_z, 0)
    state_z = []

    def send_states(m):
        szr[m, pl.ds(zl * OWN, OWN)] = szs[m, zl]
        for d in range(1, 8):
            z = lax.rem(zl + d, 8)
            state_z.append(
                go(
                    szs.at[m, z], szr.at[m, pl.ds(zl * OWN, OWN)],
                    p_s.at[m, d - 1], p_r.at[m, d - 1], at_z(z),
                )
            )

    send_states(0)
    send_states(1)
    pass_on(2)
    pass_on(1)
    w_cross.wait_recv()
    w_part = []
    for d in range(1, 8):
        p = lax.rem(part + d, 8)
        w_part.append(go(wo.at[eighth], wo.at[eighth], b_s.at[d], b_r.at[d], at_part(p)))
    pass_on(0)

    def partial(weights, first_row, i):
        total = jnp.zeros((HD, CTOK), f32)
        for n in range(13):
            total = total + jnp.dot(
                weights[rows(first_row + n * 128, 128, 128)],
                whole[pl.ds(n * 256, 256), cols[i]],
                preferred_element_type=f32,
            )
        return total

    own.wait()
    share = []
    q_cross = {}
    grad[pl.ds(HROWS, 256)] = jnp.zeros((256, HD), f32)
    for i in order:
        for cp in onward[i]:
            cp.wait_recv()
        share.append(go(whole.at[:, cols[i]], sib.at[:, cols[i]], s_s.at[i], s_r.at[i], sibling))
        if i == order[0]:
            qo[i] = partial(wt, a * (HROWS // 2), i)
            for cp in w_part:
                cp.wait_recv()
        other = partial(wo, 0, i)
        top = jnp.maximum(jnp.max(jnp.abs(other), axis=0, keepdims=True), 1e-30)
        po[i] = pack_fine(other, FINE / top)
        pm[i] = jnp.broadcast_to(top, (8, CTOK))
        q_cross[i] = [
            go(pm.at[i], pn.at[i], n_s.at[i], n_r.at[i], opposite),
            go(po.at[i], pr.at[i], q_s.at[i], q_r.at[i], opposite),
        ]
    for i in order[1:]:
        qo[i] = partial(wt, a * (HROWS // 2), i)

    factor = HD ** (-0.5)
    same = a == c
    dq_cross = []
    for i in order:
        for cp in q_cross[i]:
            cp.wait_recv()
        other = unpack_fine(pr[i], pn[i, 0:1] * (1.0 / FINE))
        queries = (qo[i] + other).T.astype(bf16)
        n = (i + 1) * CTOK
        kk = keys[pl.ds(0, n)]
        vv = values[pl.ds(0, n)]
        og = outg[cols[i]]
        scores = dot_t(queries, kk) * factor
        row_pos = lax.broadcasted_iota(jnp.int32, (CTOK, n), 0) + i * CTOK
        col_pos = lax.broadcasted_iota(jnp.int32, (CTOK, n), 1)
        scores = jnp.where(row_pos >= col_pos, scores, -1e30)
        shifted = jnp.exp(scores - jnp.max(scores, axis=1, keepdims=True))
        attention = shifted / jnp.sum(shifted, axis=1, keepdims=True)
        outputs = jnp.dot(attention.astype(bf16), vv, preferred_element_type=f32)
        deltas = jnp.sum(og.astype(f32) * outputs, axis=1, keepdims=True)
        upstream = dot_t(og, vv)
        dscores = (attention * (upstream - deltas)).astype(bf16)
        dquery = jnp.dot(dscores, kk, preferred_element_type=f32) * factor
        dqs[cols[i]] = dquery.astype(bf16)
        go(
            dqs.at[cols[i]], dqa.at[c, cols[i]], d_s.at[i], d_r.at[i, c], device(zl, y, a, 1 - a)
        )

        @pl.when(same)
        def _():
            dqa[c, cols[i]] = dqs[cols[i]]

        @pl.when(jnp.logical_not(same))
        def _():
            copy(dqs.at[cols[i]], dqa.at[c, cols[i]], h_s.at[i], h_r.at[i], sibling).start()

    send_states(2)

    def wait_dq(i):
        @pl.when(same)
        def _():
            copy(dqs.at[cols[i]], dqa.at[1 - c, cols[i]], h_s.at[i], h_r.at[i], sibling).wait_recv()

        @pl.when(jnp.logical_not(same))
        def _():
            for s in range(2):
                copy(
                    dqs.at[cols[i]], dqa.at[s, cols[i]], d_s.at[i], d_r.at[i, s], opposite
                ).wait_recv()
            copy(dqs.at[cols[i]], dqa.at[c, cols[i]], h_s.at[i], h_r.at[i], sibling).wait_send()

    def add_grad(lo, n, fresh):
        tok = pl.ds(lo, n)

        def one(j, top):
            r = rows(j * FEAT, FEAT, 16)
            g = jnp.dot(whole[r, tok], dqa[c, tok], preferred_element_type=f32)
            g = g + jnp.dot(sib[r, tok], dqa[1 - c, tok], preferred_element_type=f32)
            if not fresh:
                g = g + grad[r]
            grad[r] = g
            return jnp.maximum(top, jnp.max(jnp.abs(g), axis=0, keepdims=True))

        return lax.fori_loop(0, 4, one, jnp.zeros((1, HD), f32))

    for cp in share:
        cp.wait_recv()
    wait_dq(2)
    wait_dq(1)
    add_grad(CTOK, 2 * CTOK, True)
    wait_dq(0)
    top = add_grad(0, CTOK, False)

    e = jnp.broadcast_to(level(top), (8, HD))
    inv = inverse_of(e[:1])
    to_y = []
    for h in range(2):

        def to_fixed(k, carry):
            for j in range(OWN):
                u = (2 * k + h) * OWN + j
                r = (u // 2) * 128 + lax.rem(u, 2) * SUB
                for p in range(4):
                    ys[h, p, k * OWN + j] = pack(grad[rows(r + p * 32, SUB, SUB)], inv)
            return carry

        lax.fori_loop(0, 4, to_fixed, 0)
        for p in range(4):
            ys[h, p, 4 * OWN] = e
        for d in (1, 3, 2):
            p = lax.rem(y + d, 4)
            to_y.append(
                go(ys.at[h, p], yr.at[h, y], y_s.at[h, d - 1], y_r.at[h, d - 1], device(zl, p, c, a))
            )
        yr[h, y] = ys[h, y]

    def to_place(z):
        return copy(zs.at[z], zr.at[zl], r_s.at[z], r_r.at[zl], device(z, y, a, c))

    def from_place(z):
        return copy(zs.at[z], zr.at[z], r_s.at[z], r_r.at[z], device(z, y, a, c))

    def stays(z):
        return jnp.logical_and(same, zl == z)

    for h in range(2):
        for cp in to_y[3 * h : 3 * h + 3]:
            cp.wait_recv()
        steps = [step_of(yr[h, p, 4 * OWN, 0:1]) for p in range(4)]

        def add_y(k, top):
            for j in range(OWN):
                u = k * OWN + j
                total = unpack(yr[h, 0, u], steps[0])
                for p in range(1, 4):
                    total = total + unpack(yr[h, p, u], steps[p])
                gsum[u] = total
                top = jnp.maximum(top, jnp.max(jnp.abs(total), axis=0, keepdims=True))
            return top

        top = lax.fori_loop(0, 4, add_y, jnp.zeros((1, HD), f32))
        e = jnp.broadcast_to(level(top), (8, HD))
        inv = inverse_of(e[:1])

        def to_fixed_z(k, carry):
            for j in range(OWN):
                zs[2 * k + h, j] = pack(gsum[k * OWN + j], inv)
            zs[2 * k + h, OWN] = e
            return carry

        lax.fori_loop(0, 4, to_fixed_z, 0)
        for k in range(4):
            z = 2 * k + h

            @pl.when(stays(z))
            def _():
                zr[zl] = zs[z]

            @pl.when(jnp.logical_not(stays(z)))
            def _():
                to_place(z).start()

    for z in range(8):

        @pl.when(jnp.logical_not(stays(z)))
        def _():
            from_place(z).wait_recv()

    for cp in state_z:
        cp.wait_recv()
    steps = [step_of(zr[z, OWN, 0:1]) for z in range(8)]
    top = jnp.zeros((1, HD), f32)
    for j in range(OWN):
        total = unpack(zr[0, j], steps[0])
        for z in range(1, 8):
            total = total + unpack(zr[z, j], steps[z])
        red[j] = total
        top = jnp.maximum(top, jnp.max(jnp.abs(total), axis=0, keepdims=True))
        u = zl * OWN + j
        at = (block_code[jnp.minimum(c * HALF + u // 2, NBLK - 1)] >> 7) + j
        m_state = unpack(szr[0, at], TOP_MASTER / FIXED)
        f_state = unpack(szr[1, at], TOP_FIRST / FIXED)
        s_state = unpack(szr[2, at], TOP_SECOND / FIXED)
        nm, _, _ = adam_update(total, m_state, f_state, s_state, 1.0)
        wst[part, u] = nm.astype(bf16)

    def weights(z, p):
        return wst.at[p, pl.ds(z * OWN, OWN)]

    w_z = []
    for d in range(1, 8):
        z = lax.rem(zl + d, 8)
        w_z.append(go(weights(zl, part), weights(zl, part), w_s.at[d - 1], w_r.at[d - 1], at_z(z)))
    e = jnp.broadcast_to(level(top), (8, HD))
    inv = inverse_of(e[:1])
    for j in range(OWN):
        gq[zl * 8 + j] = pack(red[j], inv)
    gq[zl * 8 + OWN] = e
    g_z = []
    for d in range(1, 8):
        z = lax.rem(zl + d, 8)
        at = gq.at[pl.ds(zl * 8, 8)]
        g_z.append(go(at, at, a_s.at[d - 1], a_r.at[d - 1], at_z(z)))

    back_y = []
    to_core = []
    for d in range(8):
        z = lax.rem(zl - d + 8, 8)
        if d:
            w_z[d - 1].wait_recv()
        at = weights(z, part)
        back_y.append(
            [
                go(at, at, v_s.at[q - 1, d], v_r.at[q - 1, d], device(zl, lax.rem(y + q, 4), c, a))
                for q in (1, 3, 2)
            ]
        )
        to_core.append(go(at, at, c_s.at[0, d], c_r.at[0, d], sibling))

    for cp in g_z:
        cp.wait_recv()
    for p in range(8):
        for j in range(2):
            code = slot_code[zl * 16 + p * 2 + j]
            for s in range(2):
                u = (code >> (6 * s)) & 63
                send_g[p, j * 2 + s] = unpack(gq[u], step_of(gq[u | OWN][:1]))
    to_owner = []
    for d in range(1, 8):
        p = lax.rem(part + d, 8)
        to_owner.append(
            go(send_g.at[p], recv_g.at[pl.ds(part * 4, 4)], o_s.at[d - 1], o_r.at[d - 1], at_part(p))
        )
    recv_g[pl.ds(part * 4, 4)] = send_g[part]
    for d in range(8):
        z = lax.rem(zl - d + 8, 8)
        for n, q in enumerate((1, 3, 2)):
            back_y[d][n].wait_recv()
            at = weights(z, lax.rem(y - q + 4, 4) * 2 + c)
            to_core.append(go(at, at, c_s.at[q, d], c_r.at[q, d], sibling))
    for cp in to_owner:
        cp.wait_recv()
    for cp in to_core:
        cp.wait_recv()

    for z in range(8):

        @pl.when(jnp.logical_not(stays(z)))
        def _():
            to_place(z).wait_send()

    for cp in sent:
        cp.wait_send()


def finish(slot_code, parts, recv, master, first, second, out_w, out_m, out_f, out_s, recv_g, sem):
    moves = [pltpu.make_async_copy(recv, recv_g, sem.at[8])]
    for p in range(8):
        dst = out_w.at[pl.ds((p % 2) * HALF, HALF), pl.ds((p // 2) * 32, 32)]
        moves.append(pltpu.make_async_copy(parts.at[p, pl.ds(0, HALF)], dst, sem.at[p]))
    for cp in moves:
        cp.start()
    moves[0].wait()
    for j in range(2):
        code = slot_code[lax.axis_index("dp") * 2 + j]
        used = (code >> 13).astype(jnp.float32)
        h = ((code >> 12) & 1) * 4
        for n in range(4):
            for s in range(2):
                g = recv_g[h + (n * 8 + j * 2 + s)]
                r = pl.ds(n * 32 + s * SUB, SUB)
                nm, nf, ns = adam_update(g, master[j, r], first[j, r], second[j, r], used)
                out_m[j, r] = nm
                out_f[j, r] = nf
                out_s[j, r] = ns
    for cp in moves[1:]:
        cp.wait()


def body(
    activation, w_query, key_rows, value_rows, out_grad, owners, master_copy, first_moment, second_moment
):
    own_row = owners[0, :, 0]
    order = jnp.arange(NBLK, dtype=jnp.int32)
    earlier = (own_row[:, None] == own_row[None, :]) & (order[:, None] < order[None, :])
    second_slot = jnp.sum(earlier.astype(jnp.int32), axis=0)
    target = own_row * 2 + second_slot
    match = target[None, :] == jnp.arange(128, dtype=jnp.int32)[:, None]
    unit = (order % HALF) * 2
    place = (unit // OWN) * 8 + unit % OWN
    place = place + 64 * (((unit + 1) // OWN) * 8 + (unit + 1) % OWN)
    place = place + 4096 * (order // HALF) + 8192
    slot_code = jnp.sum(jnp.where(match, place[None, :], 0), axis=1)
    block_code = (own_row // 8) * (OWN * 128) + (own_row % 8) * 12 + second_slot * 2
    smem = pl.BlockSpec(memory_space=pltpu.SMEM)
    vmem = pl.BlockSpec(memory_space=pltpu.VMEM)
    anywhere = pl.BlockSpec(memory_space=pl.ANY)
    f32 = jnp.float32
    bf16 = jnp.bfloat16
    i32 = jnp.int32
    dma = pltpu.SemaphoreType.DMA

    def pair(*dims):
        return [dma(dims), dma(dims)]

    parts, gradient = pl.pallas_call(
        kernel,
        out_shape=(
            jax.ShapeDtypeStruct((8, PAD, SUB, HD), bf16),
            jax.ShapeDtypeStruct((32, SUB, HD), f32),
        ),
        in_specs=[smem] * 2 + [vmem] * 8,
        out_specs=(vmem,) * 2,
        scratch_shapes=[
            pltpu.VMEM((HROWS, TOK), bf16),
            pltpu.VMEM((HROWS, TOK), bf16),
            pltpu.VMEM((HROWS, 256), bf16),
            pltpu.VMEM((HROWS // 2, 256), bf16),
            pltpu.VMEM((CHUNKS, HD, CTOK), f32),
            pltpu.VMEM((CHUNKS, 96, CTOK), i32),
            pltpu.VMEM((CHUNKS, 96, CTOK), i32),
            pltpu.VMEM((CHUNKS, 8, CTOK), f32),
            pltpu.VMEM((CHUNKS, 8, CTOK), f32),
            pltpu.VMEM((TOK, HD), bf16),
            pltpu.VMEM((2, TOK, HD), bf16),
            pltpu.VMEM((HROWS + 256, HD), f32),
            pltpu.VMEM((2, 4, 4 * OWN + 1, 8, HD), i32),
            pltpu.VMEM((2, 4, 4 * OWN + 1, 8, HD), i32),
            pltpu.VMEM((4 * OWN, SUB, HD), f32),
            pltpu.VMEM((8, OWN + 1, 8, HD), i32),
            pltpu.VMEM((8, OWN + 1, 8, HD), i32),
            pltpu.VMEM((OWN, SUB, HD), f32),
            pltpu.VMEM((64, 8, HD), i32),
            pltpu.VMEM((8, 12, 8, HD), i32),
            pltpu.VMEM((96, 8, HD), i32),
            pltpu.VMEM((3, 8, OWN, 8, HD), i32),
            pltpu.VMEM((3, PAD, 8, HD), i32),
            pltpu.VMEM((8, 4, SUB, HD), f32),
        ]
        + pair(2, CHUNKS)
        + pair(2, CHUNKS)
        + pair(CHUNKS)
        + pair(8)
        + pair(CHUNKS)
        + pair(CHUNKS)
        + pair(CHUNKS)
        + [dma((CHUNKS,)), dma((CHUNKS, 2))]
        + pair(2, 3)
        + pair(8)
        + pair(7)
        + pair(7)
        + pair(7)
        + pair(3, 8)
        + pair(4, 8)
        + pair(7)
        + pair(3, 7)
        + [dma],
        compiler_params=pltpu.CompilerParams(
            collective_id=0, has_side_effects=True, vmem_limit_bytes=56 * 2**20
        ),
        name="project_back",
    )(
        slot_code, block_code,
        activation.T, w_query.reshape(NBLK, 128, HD), key_rows, value_rows, out_grad,
        master_copy, first_moment, second_moment,
    )
    new_w, new_m, new_f, new_s = pl.pallas_call(
        finish,
        out_shape=(
            jax.ShapeDtypeStruct((NBLK, 128, HD), bf16),
            jax.ShapeDtypeStruct((2, 128, HD), f32),
            jax.ShapeDtypeStruct((2, 128, HD), f32),
            jax.ShapeDtypeStruct((2, 128, HD), f32),
        ),
        in_specs=[smem, anywhere, anywhere] + [vmem] * 3,
        out_specs=(anywhere, vmem, vmem, vmem),
        scratch_shapes=[pltpu.VMEM((32, SUB, HD), f32), dma((9,))],
        compiler_params=pltpu.CompilerParams(vmem_limit_bytes=56 * 2**20),
        name="finish",
    )(slot_code, parts.reshape(8, PAD // 2, 2 * SUB, HD), gradient, master_copy, first_moment, second_moment)
    return (new_w.reshape(NBLK * 128, HD), new_m, new_f, new_s)


def solution(mesh):
    return jax.shard_map(
        body,
        mesh=mesh,
        in_specs=(
            P("dp", "tensor"),
            P(None, "tensor"),
            P("dp", "tensor"),
            P("dp", "tensor"),
            P("dp", "tensor"),
            P("tensor", None, None),
            P("dp", None, "tensor"),
            P("dp", None, "tensor"),
            P("dp", None, "tensor"),
        ),
        out_specs=(
            P(None, "tensor"),
            P("dp", None, "tensor"),
            P("dp", None, "tensor"),
            P("dp", None, "tensor"),
        ),
        check_vma=False,
    )
```

```python
import functools

import jax
import jax.numpy as jnp
import numpy as np
from jax import lax
from jax.experimental import pallas as pl
from jax.experimental.pallas import tpu as pltpu
from jax.sharding import PartitionSpec as P

beta_first = 0.9
beta_second = 0.95
learn_rate = 0.001
adam_eps = 1e-08
adam_step = 100.0

MESH = pl.DeviceIdType.MESH
TOK = 384
FEAT = 832
HD = 128
NBLK = 52
HALF = 26
HROWS = HALF * 128
SUB = 16
OWN = 7
PAD = 8 * OWN
CHUNKS = 3
CTOK = TOK // CHUNKS
LEVELS = 32700.0
FINE = 8388000.0
FIXED = 32766.0
TOP_MASTER = 0.078125
TOP_FIRST = 4.0
TOP_SECOND = 1.0


def adam_update(gradient, master, first, second, used):
    first_new = beta_first * first + (1.0 - beta_first) * gradient
    second_new = beta_second * second + (1.0 - beta_second) * gradient * gradient
    corr_first = 1.0 - beta_first**adam_step
    corr_second = 1.0 - beta_second**adam_step
    master_new = master - learn_rate * (first_new / corr_first) / (
        jnp.sqrt(second_new / corr_second) + adam_eps
    )
    return (master_new * used, first_new * used, second_new * used)


def dot_t(a, b):
    return lax.dot_general(a, b, (((1,), (1,)), ((), ())), preferred_element_type=jnp.float32)


def dot_0(a, b):
    return lax.dot_general(a, b, (((0,), (0,)), ((), ())), preferred_element_type=jnp.float32)


def pack(v, inv):
    q = jnp.round(v * inv).astype(jnp.int32)
    k = q.shape[0] // 2
    return (q[:k] << 16) | (q[k:] & 0xFFFF)


def unpack(u, step):
    return jnp.concatenate([u >> 16, (u << 16) >> 16], axis=0).astype(jnp.float32) * step


def pack_fine(v, inv):
    q = jnp.round(v * inv).astype(jnp.int32)
    last = q[96:]
    return jnp.concatenate(
        [
            (q[0:32] << 8) | (last & 255),
            (q[32:64] << 8) | ((last >> 8) & 255),
            (q[64:96] << 8) | ((last >> 16) & 255),
        ],
        axis=0,
    )


def unpack_fine(u, step):
    last = ((u[64:96] << 24) >> 8) | ((u[32:64] & 255) << 8) | (u[0:32] & 255)
    return jnp.concatenate([u >> 8, last], axis=0).astype(jnp.float32) * step


def level(top):
    bits = jnp.log(jnp.maximum(top, 1e-30)) * (8.0 / 0.6931471805599453)
    return jnp.ceil(bits).astype(jnp.int32)


def step_of(e):
    return jnp.exp(e.astype(jnp.float32) * (0.6931471805599453 / 8.0)) * (1.0 / LEVELS)


def inverse_of(e):
    return jnp.exp(e.astype(jnp.float32) * (-0.6931471805599453 / 8.0)) * LEVELS


def kernel(
    slot_code, block_code,
    act, w, keys, values, outg, master, first, second,
    wst, recv_g,
    whole, sib, wt, wo, qo, po, pr, pm, pn, dqs, dqa, grad, ys, yr, gsum, zs, zr, red, gq,
    sys, syr, szs, szr, send_g,
    x_s, x_r, f_s, f_r, s_s, s_r, b_s, b_r, q_s, q_r, n_s, n_r, h_s, h_r, d_s, d_r, y_s, y_r, r_s, r_r,
    a_s, a_r, o_s, o_r, w_s, w_r, v_s, v_r, c_s, c_r, k_s, k_r, p_s, p_r, l_sem,
):
    dp = lax.axis_index("dp")
    t = lax.axis_index("tensor")
    zl = dp // 8
    part = lax.rem(dp, 8)
    y = part // 2
    c = lax.rem(part, 2)
    a = t // 4
    x = lax.rem(t, 4)
    f32 = jnp.float32
    bf16 = jnp.bfloat16

    def device(z, y, c, a):
        return (z * 8 + y * 2 + c, a * 4 + x)

    def at_x(d):
        return (dp, a * 4 + lax.rem(x + d, 4))

    def at_part(p):
        return (zl * 8 + p, t)

    def at_z(z):
        return (z * 8 + part, t)

    opposite = device(zl, y, c, 1 - a)
    sibling = device(zl, y, 1 - c, a)

    def rows(start, n, unit):
        return pl.ds(pl.multiple_of(start, unit), n)

    barrier = pltpu.get_barrier_semaphore()
    peers = [at_x(d) for d in (1, 2, 3)] + [opposite]
    peers += [at_part(lax.rem(part + d, 8)) for d in range(1, 8)]
    peers += [at_z(lax.rem(zl + d, 8)) for d in range(1, 8)]
    peers += [device(lax.rem(zl + d, 8), y, 1 - c, 1 - a) for d in range(8)]
    for peer in peers:
        pl.semaphore_signal(barrier, inc=1, device_id=peer, device_id_type=MESH)

    def turn(k, carry):
        r = rows(k * 128, 128, 128)
        wt[r, 0:128] = w[k * 2].astype(f32).T.astype(bf16)
        wt[r, 128:256] = w[k * 2 + 1].astype(f32).T.astype(bf16)
        return carry

    lax.fori_loop(0, HALF, turn, 0)

    def states(p, carry):
        for j in range(2):
            for s in range(2):
                r = rows((p // 2) * 32 + s * SUB, SUB, SUB)
                n = j * 2 + s
                sys[p, n] = pack(master[j, r], FIXED / TOP_MASTER)
                sys[p, 4 + n] = pack(first[j, r], FIXED / TOP_FIRST)
                sys[p, 8 + n] = pack(second[j, r], FIXED / TOP_SECOND)
        return carry

    lax.fori_loop(0, 8, states, 0)
    pl.semaphore_wait(barrier, len(peers))
    sent = []

    def copy(src, dst, ss, rs, dev):
        return pltpu.make_async_remote_copy(
            src_ref=src, dst_ref=dst, send_sem=ss, recv_sem=rs, device_id=dev, device_id_type=MESH
        )

    def go(src, dst, ss, rs, dev):
        cp = copy(src, dst, ss, rs, dev)
        cp.start()
        sent.append(cp)
        return cp

    eighth = rows(part * 208, 208, 16)
    w_cross = go(
        wt.at[rows((1 - a) * (HROWS // 2) + part * 208, 208, 16)], wo.at[eighth],
        b_s.at[0], b_r.at[0], opposite,
    )

    cols = [pl.ds(i * CTOK, CTOK) for i in range(CHUNKS)]
    mine = rows(x * FEAT, FEAT, 16)
    own = pltpu.make_async_copy(act, whole.at[mine], l_sem)
    own.start()
    order = (2, 1, 0)
    along = {
        i: [
            go(act.at[:, cols[i]], whole.at[mine, cols[i]], x_s.at[n, i], x_r.at[n, i], at_x(d))
            for n, d in enumerate((1, 3))
        ]
        for i in order
    }
    onward = {}

    def pass_on(i):
        onward[i] = []
        for n, d in enumerate((1, 3)):
            along[i][n].wait_recv()
            r = rows(lax.rem(x - d + 4, 4) * FEAT + n * 416, 416, 16)
            at = whole.at[r, cols[i]]
            onward[i].append(go(at, at, f_s.at[n, i], f_r.at[n, i], at_x(d)))

    state_y = []
    for d in range(1, 8):
        p = lax.rem(part + d, 8)
        state_y.append(
            go(sys.at[p], syr.at[pl.ds(part * 12, 12)], k_s.at[d - 1], k_r.at[d - 1], at_part(p))
        )
    syr[pl.ds(part * 12, 12)] = sys[part]
    for cp in state_y:
        cp.wait_recv()

    def states_z(z, carry):
        for j in range(OWN):
            u = z * OWN + j
            at = (block_code[jnp.minimum(c * HALF + u // 2, NBLK - 1)] & 127) + lax.rem(u, 2)
            for m in range(3):
                szs[m, z, j] = syr[at + 4 * m]
        return carry

    lax.fori_loop(0, 8, states_z, 0)
    state_z = []

    def send_states(m):
        szr[m, pl.ds(zl * OWN, OWN)] = szs[m, zl]
        for d in range(1, 8):
            z = lax.rem(zl + d, 8)
            state_z.append(
                go(
                    szs.at[m, z], szr.at[m, pl.ds(zl * OWN, OWN)],
                    p_s.at[m, d - 1], p_r.at[m, d - 1], at_z(z),
                )
            )

    send_states(0)
    send_states(1)
    pass_on(2)
    pass_on(1)
    w_cross.wait_recv()
    w_part = []
    for d in range(1, 8):
        p = lax.rem(part + d, 8)
        w_part.append(go(wo.at[eighth], wo.at[eighth], b_s.at[d], b_r.at[d], at_part(p)))
    pass_on(0)

    def partial(weights, first_row, i):
        total = jnp.zeros((HD, CTOK), f32)
        for n in range(13):
            total = total + jnp.dot(
                weights[rows(first_row + n * 128, 128, 128)],
                whole[pl.ds(n * 256, 256), cols[i]],
                preferred_element_type=f32,
            )
        return total

    own.wait()
    share = []
    q_cross = {}
    grad[pl.ds(HROWS, 256)] = jnp.zeros((256, HD), f32)
    for i in order:
        for cp in onward[i]:
            cp.wait_recv()
        share.append(go(whole.at[:, cols[i]], sib.at[:, cols[i]], s_s.at[i], s_r.at[i], sibling))
        if i == order[0]:
            qo[i] = partial(wt, a * (HROWS // 2), i)
            for cp in w_part:
                cp.wait_recv()
        other = partial(wo, 0, i)
        top = jnp.maximum(jnp.max(jnp.abs(other), axis=0, keepdims=True), 1e-30)
        po[i] = pack_fine(other, FINE / top)
        pm[i] = jnp.broadcast_to(top, (8, CTOK))
        q_cross[i] = [
            go(pm.at[i], pn.at[i], n_s.at[i], n_r.at[i], opposite),
            go(po.at[i], pr.at[i], q_s.at[i], q_r.at[i], opposite),
        ]
    for i in order[1:]:
        qo[i] = partial(wt, a * (HROWS // 2), i)

    factor = HD ** (-0.5)
    same = a == c
    dq_cross = []
    for i in order:
        for cp in q_cross[i]:
            cp.wait_recv()
        other = unpack_fine(pr[i], pn[i, 0:1] * (1.0 / FINE))
        queries = (qo[i] + other).T.astype(bf16)
        n = (i + 1) * CTOK
        kk = keys[pl.ds(0, n)]
        vv = values[pl.ds(0, n)]
        og = outg[cols[i]]
        scores = dot_t(queries, kk) * factor
        row_pos = lax.broadcasted_iota(jnp.int32, (CTOK, n), 0) + i * CTOK
        col_pos = lax.broadcasted_iota(jnp.int32, (CTOK, n), 1)
        scores = jnp.where(row_pos >= col_pos, scores, -1e30)
        shifted = jnp.exp(scores - jnp.max(scores, axis=1, keepdims=True))
        attention = shifted / jnp.sum(shifted, axis=1, keepdims=True)
        outputs = jnp.dot(attention.astype(bf16), vv, preferred_element_type=f32)
        deltas = jnp.sum(og.astype(f32) * outputs, axis=1, keepdims=True)
        upstream = dot_t(og, vv)
        dscores = (attention * (upstream - deltas)).astype(bf16)
        dquery = jnp.dot(dscores, kk, preferred_element_type=f32) * factor
        dqs[cols[i]] = dquery.astype(bf16)
        go(
            dqs.at[cols[i]], dqa.at[c, cols[i]], d_s.at[i], d_r.at[i, c], device(zl, y, a, 1 - a)
        )

        @pl.when(same)
        def _():
            dqa[c, cols[i]] = dqs[cols[i]]

        @pl.when(jnp.logical_not(same))
        def _():
            copy(dqs.at[cols[i]], dqa.at[c, cols[i]], h_s.at[i], h_r.at[i], sibling).start()

    send_states(2)

    def wait_dq(i):
        @pl.when(same)
        def _():
            copy(dqs.at[cols[i]], dqa.at[1 - c, cols[i]], h_s.at[i], h_r.at[i], sibling).wait_recv()

        @pl.when(jnp.logical_not(same))
        def _():
            for s in range(2):
                copy(
                    dqs.at[cols[i]], dqa.at[s, cols[i]], d_s.at[i], d_r.at[i, s], opposite
                ).wait_recv()
            copy(dqs.at[cols[i]], dqa.at[c, cols[i]], h_s.at[i], h_r.at[i], sibling).wait_send()

    def add_grad(lo, n, fresh):
        tok = pl.ds(lo, n)

        def one(j, top):
            r = rows(j * FEAT, FEAT, 16)
            g = jnp.dot(whole[r, tok], dqa[c, tok], preferred_element_type=f32)
            g = g + jnp.dot(sib[r, tok], dqa[1 - c, tok], preferred_element_type=f32)
            if not fresh:
                g = g + grad[r]
            grad[r] = g
            return jnp.maximum(top, jnp.max(jnp.abs(g), axis=0, keepdims=True))

        return lax.fori_loop(0, 4, one, jnp.zeros((1, HD), f32))

    for cp in share:
        cp.wait_recv()
    wait_dq(2)
    wait_dq(1)
    add_grad(CTOK, 2 * CTOK, True)
    wait_dq(0)
    top = add_grad(0, CTOK, False)

    e = jnp.broadcast_to(level(top), (8, HD))
    inv = inverse_of(e[:1])
    to_y = []
    for h in range(2):

        def to_fixed(k, carry):
            for j in range(OWN):
                u = (2 * k + h) * OWN + j
                r = (u // 2) * 128 + lax.rem(u, 2) * SUB
                for p in range(4):
                    ys[h, p, k * OWN + j] = pack(grad[rows(r + p * 32, SUB, SUB)], inv)
            return carry

        lax.fori_loop(0, 4, to_fixed, 0)
        for p in range(4):
            ys[h, p, 4 * OWN] = e
        for d in (1, 3, 2):
            p = lax.rem(y + d, 4)
            to_y.append(
                go(ys.at[h, p], yr.at[h, y], y_s.at[h, d - 1], y_r.at[h, d - 1], device(zl, p, c, a))
            )
        yr[h, y] = ys[h, y]

    def to_place(z):
        return copy(zs.at[z], zr.at[zl], r_s.at[z], r_r.at[zl], device(z, y, a, c))

    def from_place(z):
        return copy(zs.at[z], zr.at[z], r_s.at[z], r_r.at[z], device(z, y, a, c))

    def stays(z):
        return jnp.logical_and(same, zl == z)

    for h in range(2):
        for cp in to_y[3 * h : 3 * h + 3]:
            cp.wait_recv()
        steps = [step_of(yr[h, p, 4 * OWN, 0:1]) for p in range(4)]

        def add_y(k, top):
            for j in range(OWN):
                u = k * OWN + j
                total = unpack(yr[h, 0, u], steps[0])
                for p in range(1, 4):
                    total = total + unpack(yr[h, p, u], steps[p])
                gsum[u] = total
                top = jnp.maximum(top, jnp.max(jnp.abs(total), axis=0, keepdims=True))
            return top

        top = lax.fori_loop(0, 4, add_y, jnp.zeros((1, HD), f32))
        e = jnp.broadcast_to(level(top), (8, HD))
        inv = inverse_of(e[:1])

        def to_fixed_z(k, carry):
            for j in range(OWN):
                zs[2 * k + h, j] = pack(gsum[k * OWN + j], inv)
            zs[2 * k + h, OWN] = e
            return carry

        lax.fori_loop(0, 4, to_fixed_z, 0)
        for k in range(4):
            z = 2 * k + h

            @pl.when(stays(z))
            def _():
                zr[zl] = zs[z]

            @pl.when(jnp.logical_not(stays(z)))
            def _():
                to_place(z).start()

    for z in range(8):

        @pl.when(jnp.logical_not(stays(z)))
        def _():
            from_place(z).wait_recv()

    for cp in state_z:
        cp.wait_recv()
    steps = [step_of(zr[z, OWN, 0:1]) for z in range(8)]
    top = jnp.zeros((1, HD), f32)
    for j in range(OWN):
        total = unpack(zr[0, j], steps[0])
        for z in range(1, 8):
            total = total + unpack(zr[z, j], steps[z])
        red[j] = total
        top = jnp.maximum(top, jnp.max(jnp.abs(total), axis=0, keepdims=True))
        u = zl * OWN + j
        at = (block_code[jnp.minimum(c * HALF + u // 2, NBLK - 1)] >> 7) + j
        m_state = unpack(szr[0, at], TOP_MASTER / FIXED)
        f_state = unpack(szr[1, at], TOP_FIRST / FIXED)
        s_state = unpack(szr[2, at], TOP_SECOND / FIXED)
        nm, _, _ = adam_update(total, m_state, f_state, s_state, 1.0)
        wst[part, u] = nm.astype(bf16)

    def weights(z, p):
        return wst.at[p, pl.ds(z * OWN, OWN)]

    w_z = []
    for d in range(1, 8):
        z = lax.rem(zl + d, 8)
        w_z.append(go(weights(zl, part), weights(zl, part), w_s.at[d - 1], w_r.at[d - 1], at_z(z)))
    e = jnp.broadcast_to(level(top), (8, HD))
    inv = inverse_of(e[:1])
    for j in range(OWN):
        gq[zl * 8 + j] = pack(red[j], inv)
    gq[zl * 8 + OWN] = e
    g_z = []
    for d in range(1, 8):
        z = lax.rem(zl + d, 8)
        at = gq.at[pl.ds(zl * 8, 8)]
        g_z.append(go(at, at, a_s.at[d - 1], a_r.at[d - 1], at_z(z)))

    back_y = []
    to_core = []
    for d in range(8):
        z = lax.rem(zl - d + 8, 8)
        if d:
            w_z[d - 1].wait_recv()
        at = weights(z, part)
        back_y.append(
            [
                go(at, at, v_s.at[q - 1, d], v_r.at[q - 1, d], device(zl, lax.rem(y + q, 4), c, a))
                for q in (1, 3, 2)
            ]
        )
        to_core.append(go(at, at, c_s.at[0, d], c_r.at[0, d], sibling))

    for cp in g_z:
        cp.wait_recv()
    for p in range(8):
        for j in range(2):
            code = slot_code[zl * 16 + p * 2 + j]
            for s in range(2):
                u = (code >> (6 * s)) & 63
                send_g[p, j * 2 + s] = unpack(gq[u], step_of(gq[u | OWN][:1]))
    to_owner = []
    for d in range(1, 8):
        p = lax.rem(part + d, 8)
        to_owner.append(
            go(send_g.at[p], recv_g.at[pl.ds(part * 4, 4)], o_s.at[d - 1], o_r.at[d - 1], at_part(p))
        )
    recv_g[pl.ds(part * 4, 4)] = send_g[part]
    for d in range(8):
        z = lax.rem(zl - d + 8, 8)
        for n, q in enumerate((1, 3, 2)):
            back_y[d][n].wait_recv()
            at = weights(z, lax.rem(y - q + 4, 4) * 2 + c)
            to_core.append(go(at, at, c_s.at[q, d], c_r.at[q, d], sibling))
    for cp in to_owner:
        cp.wait_recv()
    for cp in to_core:
        cp.wait_recv()

    for z in range(8):

        @pl.when(jnp.logical_not(stays(z)))
        def _():
            to_place(z).wait_send()

    for cp in sent:
        cp.wait_send()


def finish(slot_code, parts, recv, master, first, second, out_w, out_m, out_f, out_s, recv_g, sem):
    moves = [pltpu.make_async_copy(recv, recv_g, sem.at[8])]
    for p in range(8):
        dst = out_w.at[pl.ds((p % 2) * HALF, HALF), pl.ds((p // 2) * 32, 32)]
        moves.append(pltpu.make_async_copy(parts.at[p, pl.ds(0, HALF)], dst, sem.at[p]))
    for cp in moves:
        cp.start()
    moves[0].wait()
    for j in range(2):
        code = slot_code[lax.axis_index("dp") * 2 + j]
        used = (code >> 13).astype(jnp.float32)
        h = ((code >> 12) & 1) * 4
        for n in range(4):
            for s in range(2):
                g = recv_g[h + (n * 8 + j * 2 + s)]
                r = pl.ds(n * 32 + s * SUB, SUB)
                nm, nf, ns = adam_update(g, master[j, r], first[j, r], second[j, r], used)
                out_m[j, r] = nm
                out_f[j, r] = nf
                out_s[j, r] = ns
    for cp in moves[1:]:
        cp.wait()


def body(
    activation, w_query, key_rows, value_rows, out_grad, owners, master_copy, first_moment, second_moment
):
    own_row = owners[0, :, 0]
    order = np.arange(NBLK, dtype=np.int32)
    unit = (order % HALF) * 2
    place = (unit // OWN) * 8 + unit % OWN
    place = place + 64 * (((unit + 1) // OWN) * 8 + (unit + 1) % OWN)
    place = place + 4096 * (order // HALF) + 8192
    keyed = jnp.asarray(order * 65536 + place, jnp.int32)
    slots = np.arange(128, dtype=np.int32)
    match = own_row[None, :] == jnp.asarray(slots[:, None] >> 1)
    lowest = jnp.min(jnp.where(match, keyed[None, :], 1 << 30), axis=1)
    highest = jnp.max(jnp.where(match, keyed[None, :], -1), axis=1)
    upper = jnp.asarray((slots & 1) == 1)
    there = jnp.where(upper, highest > lowest, highest >= 0)
    slot_code = jnp.where(there, jnp.where(upper, highest, lowest) & 65535, 0)
    earlier = (own_row[:, None] == own_row[None, :]) & jnp.asarray(order[None, :] < order[:, None])
    second_slot = jnp.sum(earlier.astype(jnp.int32), axis=1)
    block_code = (own_row >> 3) * (OWN * 128) + (own_row & 7) * 12 + second_slot * 2
    smem = pl.BlockSpec(memory_space=pltpu.SMEM)
    vmem = pl.BlockSpec(memory_space=pltpu.VMEM)
    anywhere = pl.BlockSpec(memory_space=pl.ANY)
    f32 = jnp.float32
    bf16 = jnp.bfloat16
    i32 = jnp.int32
    dma = pltpu.SemaphoreType.DMA

    def pair(*dims):
        return [dma(dims), dma(dims)]

    parts, gradient = pl.pallas_call(
        kernel,
        out_shape=(
            jax.ShapeDtypeStruct((8, PAD, SUB, HD), bf16),
            jax.ShapeDtypeStruct((32, SUB, HD), f32),
        ),
        in_specs=[smem] * 2 + [vmem] * 8,
        out_specs=(vmem,) * 2,
        scratch_shapes=[
            pltpu.VMEM((HROWS, TOK), bf16),
            pltpu.VMEM((HROWS, TOK), bf16),
            pltpu.VMEM((HROWS, 256), bf16),
            pltpu.VMEM((HROWS // 2, 256), bf16),
            pltpu.VMEM((CHUNKS, HD, CTOK), f32),
            pltpu.VMEM((CHUNKS, 96, CTOK), i32),
            pltpu.VMEM((CHUNKS, 96, CTOK), i32),
            pltpu.VMEM((CHUNKS, 8, CTOK), f32),
            pltpu.VMEM((CHUNKS, 8, CTOK), f32),
            pltpu.VMEM((TOK, HD), bf16),
            pltpu.VMEM((2, TOK, HD), bf16),
            pltpu.VMEM((HROWS + 256, HD), f32),
            pltpu.VMEM((2, 4, 4 * OWN + 1, 8, HD), i32),
            pltpu.VMEM((2, 4, 4 * OWN + 1, 8, HD), i32),
            pltpu.VMEM((4 * OWN, SUB, HD), f32),
            pltpu.VMEM((8, OWN + 1, 8, HD), i32),
            pltpu.VMEM((8, OWN + 1, 8, HD), i32),
            pltpu.VMEM((OWN, SUB, HD), f32),
            pltpu.VMEM((64, 8, HD), i32),
            pltpu.VMEM((8, 12, 8, HD), i32),
            pltpu.VMEM((96, 8, HD), i32),
            pltpu.VMEM((3, 8, OWN, 8, HD), i32),
            pltpu.VMEM((3, PAD, 8, HD), i32),
            pltpu.VMEM((8, 4, SUB, HD), f32),
        ]
        + pair(2, CHUNKS)
        + pair(2, CHUNKS)
        + pair(CHUNKS)
        + pair(8)
        + pair(CHUNKS)
        + pair(CHUNKS)
        + pair(CHUNKS)
        + [dma((CHUNKS,)), dma((CHUNKS, 2))]
        + pair(2, 3)
        + pair(8)
        + pair(7)
        + pair(7)
        + pair(7)
        + pair(3, 8)
        + pair(4, 8)
        + pair(7)
        + pair(3, 7)
        + [dma],
        compiler_params=pltpu.CompilerParams(
            collective_id=0, has_side_effects=True, vmem_limit_bytes=56 * 2**20
        ),
        name="project_back",
    )(
        slot_code, block_code,
        activation.T, w_query.reshape(NBLK, 128, HD), key_rows, value_rows, out_grad,
        master_copy, first_moment, second_moment,
    )
    new_w, new_m, new_f, new_s = pl.pallas_call(
        finish,
        out_shape=(
            jax.ShapeDtypeStruct((NBLK, 128, HD), bf16),
            jax.ShapeDtypeStruct((2, 128, HD), f32),
            jax.ShapeDtypeStruct((2, 128, HD), f32),
            jax.ShapeDtypeStruct((2, 128, HD), f32),
        ),
        in_specs=[smem, anywhere, anywhere] + [vmem] * 3,
        out_specs=(vmem,) * 4,
        scratch_shapes=[pltpu.VMEM((32, SUB, HD), f32), dma((9,))],
        compiler_params=pltpu.CompilerParams(vmem_limit_bytes=56 * 2**20),
        name="finish",
    )(slot_code, parts.reshape(8, PAD // 2, 2 * SUB, HD), gradient, master_copy, first_moment, second_moment)
    return (new_w.reshape(NBLK * 128, HD), new_m, new_f, new_s)


def solution(mesh):
    return jax.shard_map(
        body,
        mesh=mesh,
        in_specs=(
            P("dp", "tensor"),
            P(None, "tensor"),
            P("dp", "tensor"),
            P("dp", "tensor"),
            P("dp", "tensor"),
            P("tensor", None, None),
            P("dp", None, "tensor"),
            P("dp", None, "tensor"),
            P("dp", None, "tensor"),
        ),
        out_specs=(
            P(None, "tensor"),
            P("dp", None, "tensor"),
            P("dp", None, "tensor"),
            P("dp", None, "tensor"),
        ),
        check_vma=False,
    )
```

```python
import functools

import jax
import jax.numpy as jnp
from jax import lax
from jax.experimental import pallas as pl
from jax.experimental.pallas import tpu as pltpu
from jax.sharding import PartitionSpec as P

beta_first = 0.9
beta_second = 0.95
learn_rate = 0.001
adam_eps = 1e-08
adam_step = 100.0

MESH = pl.DeviceIdType.MESH
TOK = 384
FEAT = 832
HD = 128
NBLK = 52
HALF = 26
HROWS = HALF * 128
SUB = 16
OWN = 7
PAD = 8 * OWN
CHUNKS = 3
CTOK = TOK // CHUNKS
LEVELS = 32700.0
FINE = 8388000.0
FIXED = 32766.0
TOP_MASTER = 0.078125
TOP_FIRST = 4.0
TOP_SECOND = 1.0


def adam_update(gradient, master, first, second, used):
    first_new = beta_first * first + (1.0 - beta_first) * gradient
    second_new = beta_second * second + (1.0 - beta_second) * gradient * gradient
    corr_first = 1.0 - beta_first**adam_step
    corr_second = 1.0 - beta_second**adam_step
    master_new = master - learn_rate * (first_new / corr_first) / (
        jnp.sqrt(second_new / corr_second) + adam_eps
    )
    return (master_new * used, first_new * used, second_new * used)


def dot_t(a, b):
    return lax.dot_general(a, b, (((1,), (1,)), ((), ())), preferred_element_type=jnp.float32)


def dot_0(a, b):
    return lax.dot_general(a, b, (((0,), (0,)), ((), ())), preferred_element_type=jnp.float32)


def pack(v, inv):
    q = jnp.round(v * inv).astype(jnp.int32)
    k = q.shape[0] // 2
    return (q[:k] << 16) | (q[k:] & 0xFFFF)


def unpack(u, step):
    return jnp.concatenate([u >> 16, (u << 16) >> 16], axis=0).astype(jnp.float32) * step


def pack_fine(v, inv):
    q = jnp.round(v * inv).astype(jnp.int32)
    last = q[96:]
    return jnp.concatenate(
        [
            (q[0:32] << 8) | (last & 255),
            (q[32:64] << 8) | ((last >> 8) & 255),
            (q[64:96] << 8) | ((last >> 16) & 255),
        ],
        axis=0,
    )


def unpack_fine(u, step):
    last = ((u[64:96] << 24) >> 8) | ((u[32:64] & 255) << 8) | (u[0:32] & 255)
    return jnp.concatenate([u >> 8, last], axis=0).astype(jnp.float32) * step


def level(top):
    bits = jnp.log(jnp.maximum(top, 1e-30)) * (8.0 / 0.6931471805599453)
    return jnp.ceil(bits).astype(jnp.int32)


def step_of(e):
    return jnp.exp(e.astype(jnp.float32) * (0.6931471805599453 / 8.0)) * (1.0 / LEVELS)


def inverse_of(e):
    return jnp.exp(e.astype(jnp.float32) * (-0.6931471805599453 / 8.0)) * LEVELS


def kernel(
    slot_code, block_code,
    act, w, keys, values, outg, master, first, second,
    wst, recv_g,
    whole, sib, wt, wo, qo, po, pr, pm, pn, dqs, dqa, grad, ys, yr, gsum, zs, zr, red, gq,
    sys, syr, szs, szr, send_g,
    x_s, x_r, f_s, f_r, s_s, s_r, b_s, b_r, q_s, q_r, n_s, n_r, h_s, h_r, d_s, d_r, y_s, y_r, r_s, r_r,
    a_s, a_r, o_s, o_r, w_s, w_r, v_s, v_r, c_s, c_r, k_s, k_r, p_s, p_r, l_sem,
):
    dp = lax.axis_index("dp")
    t = lax.axis_index("tensor")
    zl = dp // 8
    part = lax.rem(dp, 8)
    y = part // 2
    c = lax.rem(part, 2)
    a = t // 4
    x = lax.rem(t, 4)
    f32 = jnp.float32
    bf16 = jnp.bfloat16

    def device(z, y, c, a):
        return (z * 8 + y * 2 + c, a * 4 + x)

    def at_x(d):
        return (dp, a * 4 + lax.rem(x + d, 4))

    def at_part(p):
        return (zl * 8 + p, t)

    def at_z(z):
        return (z * 8 + part, t)

    opposite = device(zl, y, c, 1 - a)
    sibling = device(zl, y, 1 - c, a)

    def rows(start, n, unit):
        return pl.ds(pl.multiple_of(start, unit), n)

    barrier = pltpu.get_barrier_semaphore()
    peers = [at_x(d) for d in (1, 2, 3)] + [opposite]
    peers += [at_part(lax.rem(part + d, 8)) for d in range(1, 8)]
    peers += [at_z(lax.rem(zl + d, 8)) for d in range(1, 8)]
    peers += [device(lax.rem(zl + d, 8), y, 1 - c, 1 - a) for d in range(8)]
    for peer in peers:
        pl.semaphore_signal(barrier, inc=1, device_id=peer, device_id_type=MESH)

    def turn(k, carry):
        r = rows(k * 128, 128, 128)
        wt[r, 0:128] = w[k * 2].astype(f32).T.astype(bf16)
        wt[r, 128:256] = w[k * 2 + 1].astype(f32).T.astype(bf16)
        return carry

    lax.fori_loop(0, HALF, turn, 0)

    def states(p, carry):
        for j in range(2):
            for s in range(2):
                r = rows((p // 2) * 32 + s * SUB, SUB, SUB)
                n = j * 2 + s
                sys[p, n] = pack(master[j, r], FIXED / TOP_MASTER)
                sys[p, 4 + n] = pack(first[j, r], FIXED / TOP_FIRST)
                sys[p, 8 + n] = pack(second[j, r], FIXED / TOP_SECOND)
        return carry

    lax.fori_loop(0, 8, states, 0)
    pl.semaphore_wait(barrier, len(peers))
    sent = []

    def copy(src, dst, ss, rs, dev):
        return pltpu.make_async_remote_copy(
            src_ref=src, dst_ref=dst, send_sem=ss, recv_sem=rs, device_id=dev, device_id_type=MESH
        )

    def go(src, dst, ss, rs, dev):
        cp = copy(src, dst, ss, rs, dev)
        cp.start()
        sent.append(cp)
        return cp

    eighth = rows(part * 208, 208, 16)
    w_cross = go(
        wt.at[rows((1 - a) * (HROWS // 2) + part * 208, 208, 16)], wo.at[eighth],
        b_s.at[0], b_r.at[0], opposite,
    )

    cols = [pl.ds(i * CTOK, CTOK) for i in range(CHUNKS)]
    mine = rows(x * FEAT, FEAT, 16)
    own = pltpu.make_async_copy(act, whole.at[mine], l_sem)
    own.start()
    order = (2, 1, 0)
    along = {
        i: [
            go(act.at[:, cols[i]], whole.at[mine, cols[i]], x_s.at[n, i], x_r.at[n, i], at_x(d))
            for n, d in enumerate((1, 3))
        ]
        for i in order
    }
    onward = {}

    def pass_on(i):
        onward[i] = []
        for n, d in enumerate((1, 3)):
            along[i][n].wait_recv()
            r = rows(lax.rem(x - d + 4, 4) * FEAT + n * 416, 416, 16)
            at = whole.at[r, cols[i]]
            onward[i].append(go(at, at, f_s.at[n, i], f_r.at[n, i], at_x(d)))

    state_y = []
    for d in range(1, 8):
        p = lax.rem(part + d, 8)
        state_y.append(
            go(sys.at[p], syr.at[pl.ds(part * 12, 12)], k_s.at[d - 1], k_r.at[d - 1], at_part(p))
        )
    syr[pl.ds(part * 12, 12)] = sys[part]
    for cp in state_y:
        cp.wait_recv()

    def states_z(z, carry):
        for j in range(OWN):
            u = z * OWN + j
            at = (block_code[jnp.minimum(c * HALF + u // 2, NBLK - 1)] & 127) + lax.rem(u, 2)
            for m in range(3):
                szs[m, z, j] = syr[at + 4 * m]
        return carry

    lax.fori_loop(0, 8, states_z, 0)
    state_z = []

    def send_states(m):
        szr[m, pl.ds(zl * OWN, OWN)] = szs[m, zl]
        for d in range(1, 8):
            z = lax.rem(zl + d, 8)
            state_z.append(
                go(
                    szs.at[m, z], szr.at[m, pl.ds(zl * OWN, OWN)],
                    p_s.at[m, d - 1], p_r.at[m, d - 1], at_z(z),
                )
            )

    send_states(0)
    send_states(1)
    pass_on(2)
    pass_on(1)
    w_cross.wait_recv()
    w_part = []
    for d in range(1, 8):
        p = lax.rem(part + d, 8)
        w_part.append(go(wo.at[eighth], wo.at[eighth], b_s.at[d], b_r.at[d], at_part(p)))
    pass_on(0)

    def partial(weights, first_row, i):
        total = jnp.zeros((HD, CTOK), f32)
        for n in range(13):
            total = total + jnp.dot(
                weights[rows(first_row + n * 128, 128, 128)],
                whole[pl.ds(n * 256, 256), cols[i]],
                preferred_element_type=f32,
            )
        return total

    own.wait()
    share = []
    q_cross = {}
    grad[pl.ds(HROWS, 256)] = jnp.zeros((256, HD), f32)
    for i in order:
        for cp in onward[i]:
            cp.wait_recv()
        share.append(go(whole.at[:, cols[i]], sib.at[:, cols[i]], s_s.at[i], s_r.at[i], sibling))
        if i == order[0]:
            qo[i] = partial(wt, a * (HROWS // 2), i)
            for cp in w_part:
                cp.wait_recv()
        other = partial(wo, 0, i)
        top = jnp.maximum(jnp.max(jnp.abs(other), axis=0, keepdims=True), 1e-30)
        po[i] = pack_fine(other, FINE / top)
        pm[i] = jnp.broadcast_to(top, (8, CTOK))
        q_cross[i] = [
            go(pm.at[i], pn.at[i], n_s.at[i], n_r.at[i], opposite),
            go(po.at[i], pr.at[i], q_s.at[i], q_r.at[i], opposite),
        ]
    for i in order[1:]:
        qo[i] = partial(wt, a * (HROWS // 2), i)

    factor = HD ** (-0.5)
    same = a == c
    dq_cross = []
    for i in order:
        for cp in q_cross[i]:
            cp.wait_recv()
        other = unpack_fine(pr[i], pn[i, 0:1] * (1.0 / FINE))
        queries = (qo[i] + other).T.astype(bf16)
        n = (i + 1) * CTOK
        kk = keys[pl.ds(0, n)]
        vv = values[pl.ds(0, n)]
        og = outg[cols[i]]
        scores = dot_t(queries, kk) * factor
        row_pos = lax.broadcasted_iota(jnp.int32, (CTOK, n), 0) + i * CTOK
        col_pos = lax.broadcasted_iota(jnp.int32, (CTOK, n), 1)
        scores = jnp.where(row_pos >= col_pos, scores, -1e30)
        shifted = jnp.exp(scores - jnp.max(scores, axis=1, keepdims=True))
        attention = shifted / jnp.sum(shifted, axis=1, keepdims=True)
        outputs = jnp.dot(attention.astype(bf16), vv, preferred_element_type=f32)
        deltas = jnp.sum(og.astype(f32) * outputs, axis=1, keepdims=True)
        upstream = dot_t(og, vv)
        dscores = (attention * (upstream - deltas)).astype(bf16)
        dquery = jnp.dot(dscores, kk, preferred_element_type=f32) * factor
        dqs[cols[i]] = dquery.astype(bf16)
        go(
            dqs.at[cols[i]], dqa.at[c, cols[i]], d_s.at[i], d_r.at[i, c], device(zl, y, a, 1 - a)
        )

        @pl.when(same)
        def _():
            dqa[c, cols[i]] = dqs[cols[i]]

        @pl.when(jnp.logical_not(same))
        def _():
            copy(dqs.at[cols[i]], dqa.at[c, cols[i]], h_s.at[i], h_r.at[i], sibling).start()

    send_states(2)

    def wait_dq(i):
        @pl.when(same)
        def _():
            copy(dqs.at[cols[i]], dqa.at[1 - c, cols[i]], h_s.at[i], h_r.at[i], sibling).wait_recv()

        @pl.when(jnp.logical_not(same))
        def _():
            for s in range(2):
                copy(
                    dqs.at[cols[i]], dqa.at[s, cols[i]], d_s.at[i], d_r.at[i, s], opposite
                ).wait_recv()
            copy(dqs.at[cols[i]], dqa.at[c, cols[i]], h_s.at[i], h_r.at[i], sibling).wait_send()

    def add_grad(lo, n, fresh):
        tok = pl.ds(lo, n)

        def one(j, top):
            r = rows(j * FEAT, FEAT, 16)
            g = jnp.dot(whole[r, tok], dqa[c, tok], preferred_element_type=f32)
            g = g + jnp.dot(sib[r, tok], dqa[1 - c, tok], preferred_element_type=f32)
            if not fresh:
                g = g + grad[r]
            grad[r] = g
            return jnp.maximum(top, jnp.max(jnp.abs(g), axis=0, keepdims=True))

        return lax.fori_loop(0, 4, one, jnp.zeros((1, HD), f32))

    for cp in share:
        cp.wait_recv()
    wait_dq(2)
    wait_dq(1)
    add_grad(CTOK, 2 * CTOK, True)
    wait_dq(0)
    top = add_grad(0, CTOK, False)

    e = jnp.broadcast_to(level(top), (8, HD))
    inv = inverse_of(e[:1])
    to_y = []
    for h in range(2):

        def to_fixed(k, carry):
            for j in range(OWN):
                u = (2 * k + h) * OWN + j
                r = (u // 2) * 128 + lax.rem(u, 2) * SUB
                for p in range(4):
                    ys[h, p, k * OWN + j] = pack(grad[rows(r + p * 32, SUB, SUB)], inv)
            return carry

        lax.fori_loop(0, 4, to_fixed, 0)
        for p in range(4):
            ys[h, p, 4 * OWN] = e
        for d in (1, 3, 2):
            p = lax.rem(y + d, 4)
            to_y.append(
                go(ys.at[h, p], yr.at[h, y], y_s.at[h, d - 1], y_r.at[h, d - 1], device(zl, p, c, a))
            )
        yr[h, y] = ys[h, y]

    def to_place(z):
        return copy(zs.at[z], zr.at[zl], r_s.at[z], r_r.at[zl], device(z, y, a, c))

    def from_place(z):
        return copy(zs.at[z], zr.at[z], r_s.at[z], r_r.at[z], device(z, y, a, c))

    def stays(z):
        return jnp.logical_and(same, zl == z)

    for h in range(2):
        for cp in to_y[3 * h : 3 * h + 3]:
            cp.wait_recv()
        steps = [step_of(yr[h, p, 4 * OWN, 0:1]) for p in range(4)]

        def add_y(k, carry):
            for j in range(OWN):
                u = k * OWN + j
                total = unpack(yr[h, 0, u], steps[0])
                for p in range(1, 4):
                    total = total + unpack(yr[h, p, u], steps[p])
                gsum[u] = total
            return carry

        lax.fori_loop(0, 4, add_y, 0)
        e = jnp.broadcast_to(level(LEVELS * (steps[0] + steps[1] + steps[2] + steps[3])), (8, HD))
        inv = inverse_of(e[:1])

        def to_fixed_z(k, carry):
            for j in range(OWN):
                zs[2 * k + h, j] = pack(gsum[k * OWN + j], inv)
            zs[2 * k + h, OWN] = e
            return carry

        lax.fori_loop(0, 4, to_fixed_z, 0)
        for k in range(4):
            z = 2 * k + h

            @pl.when(stays(z))
            def _():
                zr[zl] = zs[z]

            @pl.when(jnp.logical_not(stays(z)))
            def _():
                to_place(z).start()

    for z in range(8):

        @pl.when(jnp.logical_not(stays(z)))
        def _():
            from_place(z).wait_recv()

    for cp in state_z:
        cp.wait_recv()
    steps = [step_of(zr[z, OWN, 0:1]) for z in range(8)]
    for j in range(OWN):
        total = unpack(zr[0, j], steps[0])
        for z in range(1, 8):
            total = total + unpack(zr[z, j], steps[z])
        red[j] = total
        u = zl * OWN + j
        at = (block_code[jnp.minimum(c * HALF + u // 2, NBLK - 1)] >> 7) + j
        m_state = unpack(szr[0, at], TOP_MASTER / FIXED)
        f_state = unpack(szr[1, at], TOP_FIRST / FIXED)
        s_state = unpack(szr[2, at], TOP_SECOND / FIXED)
        nm, _, _ = adam_update(total, m_state, f_state, s_state, 1.0)
        wst[part, u] = nm.astype(bf16)

    def weights(z, p):
        return wst.at[p, pl.ds(z * OWN, OWN)]

    w_z = []
    for d in range(1, 8):
        z = lax.rem(zl + d, 8)
        w_z.append(go(weights(zl, part), weights(zl, part), w_s.at[d - 1], w_r.at[d - 1], at_z(z)))
    bound = steps[0]
    for z in range(1, 8):
        bound = bound + steps[z]
    e = level(LEVELS * bound)
    inv = inverse_of(e)
    g_step = step_of(e)
    for j in range(OWN):
        gq[zl * OWN + j] = pack(red[j], inv)
    g_z = []
    for d in range(1, 8):
        z = lax.rem(zl + d, 8)
        at = gq.at[pl.ds(zl * OWN, OWN)]
        g_z.append(go(at, at, a_s.at[d - 1], a_r.at[d - 1], at_z(z)))

    back_y = []
    to_core = []
    for d in range(8):
        z = lax.rem(zl - d + 8, 8)
        if d:
            w_z[d - 1].wait_recv()
        at = weights(z, part)
        back_y.append(
            [
                go(at, at, v_s.at[q - 1, d], v_r.at[q - 1, d], device(zl, lax.rem(y + q, 4), c, a))
                for q in (1, 3, 2)
            ]
        )
        to_core.append(go(at, at, c_s.at[0, d], c_r.at[0, d], sibling))

    for cp in g_z:
        cp.wait_recv()
    for p in range(8):
        for j in range(2):
            code = slot_code[zl * 16 + p * 2 + j]
            for s in range(2):
                u = (code >> (6 * s)) & 63
                send_g[p, j * 2 + s] = unpack(gq[u], g_step)
    to_owner = []
    for d in range(1, 8):
        p = lax.rem(part + d, 8)
        to_owner.append(
            go(send_g.at[p], recv_g.at[pl.ds(part * 4, 4)], o_s.at[d - 1], o_r.at[d - 1], at_part(p))
        )
    recv_g[pl.ds(part * 4, 4)] = send_g[part]
    for d in range(8):
        z = lax.rem(zl - d + 8, 8)
        for n, q in enumerate((1, 3, 2)):
            back_y[d][n].wait_recv()
            at = weights(z, lax.rem(y - q + 4, 4) * 2 + c)
            to_core.append(go(at, at, c_s.at[q, d], c_r.at[q, d], sibling))
    for cp in to_owner:
        cp.wait_recv()
    for cp in to_core:
        cp.wait_recv()

    for z in range(8):

        @pl.when(jnp.logical_not(stays(z)))
        def _():
            to_place(z).wait_send()

    for cp in sent:
        cp.wait_send()


def finish(slot_code, parts, recv, master, first, second, out_w, out_m, out_f, out_s, recv_g, held, sem):
    moves = [pltpu.make_async_copy(recv, recv_g, sem.at[8])]
    for p in range(8):
        moves.append(pltpu.make_async_copy(parts.at[p], held.at[p], sem.at[p]))
    for cp in moves:
        cp.start()
    moves[0].wait()
    for j in range(2):
        code = slot_code[lax.axis_index("dp") * 2 + j]
        used = (code >> 13).astype(jnp.float32)
        h = ((code >> 12) & 1) * 4
        for n in range(4):
            for s in range(2):
                g = recv_g[h + (n * 8 + j * 2 + s)]
                r = pl.ds(n * 32 + s * SUB, SUB)
                nm, nf, ns = adam_update(g, master[j, r], first[j, r], second[j, r], used)
                out_m[j, r] = nm
                out_f[j, r] = nf
                out_s[j, r] = ns
    for p in range(8):
        moves[1 + p].wait()
        b = (p % 2) * HALF
        r = (p // 2) * 32
        out_w[b : b + HALF, r : r + 32] = held[p, 0:HALF]


def body(
    activation, w_query, key_rows, value_rows, out_grad, owners, master_copy, first_moment, second_moment
):
    own_row = owners[0, :, 0]
    order = jnp.arange(NBLK, dtype=jnp.int32)
    earlier = (own_row[:, None] == own_row[None, :]) & (order[:, None] < order[None, :])
    second_slot = jnp.sum(earlier.astype(jnp.int32), axis=0)
    target = own_row * 2 + second_slot
    match = target[None, :] == jnp.arange(128, dtype=jnp.int32)[:, None]
    unit = (order % HALF) * 2
    place = unit
    place = place + 64 * (unit + 1)
    place = place + 4096 * (order // HALF) + 8192
    slot_code = jnp.sum(jnp.where(match, place[None, :], 0), axis=1)
    block_code = (own_row >> 3) * (OWN * 128) + (own_row & 7) * 12 + second_slot * 2
    smem = pl.BlockSpec(memory_space=pltpu.SMEM)
    vmem = pl.BlockSpec(memory_space=pltpu.VMEM)
    anywhere = pl.BlockSpec(memory_space=pl.ANY)
    f32 = jnp.float32
    bf16 = jnp.bfloat16
    i32 = jnp.int32
    dma = pltpu.SemaphoreType.DMA

    def pair(*dims):
        return [dma(dims), dma(dims)]

    parts, gradient = pl.pallas_call(
        kernel,
        out_shape=(
            jax.ShapeDtypeStruct((8, PAD, SUB, HD), bf16),
            jax.ShapeDtypeStruct((32, SUB, HD), f32),
        ),
        in_specs=[smem] * 2 + [vmem] * 8,
        out_specs=(vmem,) * 2,
        scratch_shapes=[
            pltpu.VMEM((HROWS, TOK), bf16),
            pltpu.VMEM((HROWS, TOK), bf16),
            pltpu.VMEM((HROWS, 256), bf16),
            pltpu.VMEM((HROWS // 2, 256), bf16),
            pltpu.VMEM((CHUNKS, HD, CTOK), f32),
            pltpu.VMEM((CHUNKS, 96, CTOK), i32),
            pltpu.VMEM((CHUNKS, 96, CTOK), i32),
            pltpu.VMEM((CHUNKS, 8, CTOK), f32),
            pltpu.VMEM((CHUNKS, 8, CTOK), f32),
            pltpu.VMEM((TOK, HD), bf16),
            pltpu.VMEM((2, TOK, HD), bf16),
            pltpu.VMEM((HROWS + 256, HD), f32),
            pltpu.VMEM((2, 4, 4 * OWN + 1, 8, HD), i32),
            pltpu.VMEM((2, 4, 4 * OWN + 1, 8, HD), i32),
            pltpu.VMEM((4 * OWN, SUB, HD), f32),
            pltpu.VMEM((8, OWN + 1, 8, HD), i32),
            pltpu.VMEM((8, OWN + 1, 8, HD), i32),
            pltpu.VMEM((OWN, SUB, HD), f32),
            pltpu.VMEM((PAD, 8, HD), i32),
            pltpu.VMEM((8, 12, 8, HD), i32),
            pltpu.VMEM((96, 8, HD), i32),
            pltpu.VMEM((3, 8, OWN, 8, HD), i32),
            pltpu.VMEM((3, PAD, 8, HD), i32),
            pltpu.VMEM((8, 4, SUB, HD), f32),
        ]
        + pair(2, CHUNKS)
        + pair(2, CHUNKS)
        + pair(CHUNKS)
        + pair(8)
        + pair(CHUNKS)
        + pair(CHUNKS)
        + pair(CHUNKS)
        + [dma((CHUNKS,)), dma((CHUNKS, 2))]
        + pair(2, 3)
        + pair(8)
        + pair(7)
        + pair(7)
        + pair(7)
        + pair(3, 8)
        + pair(4, 8)
        + pair(7)
        + pair(3, 7)
        + [dma],
        compiler_params=pltpu.CompilerParams(
            collective_id=0, has_side_effects=True, vmem_limit_bytes=56 * 2**20
        ),
        name="project_back",
    )(
        slot_code, block_code,
        activation.T, w_query.reshape(NBLK, 128, HD), key_rows, value_rows, out_grad,
        master_copy, first_moment, second_moment,
    )
    new_w, new_m, new_f, new_s = pl.pallas_call(
        finish,
        out_shape=(
            jax.ShapeDtypeStruct((NBLK, 128, HD), bf16),
            jax.ShapeDtypeStruct((2, 128, HD), f32),
            jax.ShapeDtypeStruct((2, 128, HD), f32),
            jax.ShapeDtypeStruct((2, 128, HD), f32),
        ),
        in_specs=[smem, anywhere, anywhere] + [vmem] * 3,
        out_specs=(vmem,) * 4,
        scratch_shapes=[
            pltpu.VMEM((32, SUB, HD), f32),
            pltpu.VMEM((8, PAD // 2, 2 * SUB, HD), bf16),
            dma((9,)),
        ],
        compiler_params=pltpu.CompilerParams(vmem_limit_bytes=56 * 2**20),
        name="finish",
    )(slot_code, parts.reshape(8, PAD // 2, 2 * SUB, HD), gradient, master_copy, first_moment, second_moment)
    return (new_w.reshape(NBLK * 128, HD), new_m, new_f, new_s)


def solution(mesh):
    return jax.shard_map(
        body,
        mesh=mesh,
        in_specs=(
            P("dp", "tensor"),
            P(None, "tensor"),
            P("dp", "tensor"),
            P("dp", "tensor"),
            P("dp", "tensor"),
            P("tensor", None, None),
            P("dp", None, "tensor"),
            P("dp", None, "tensor"),
            P("dp", None, "tensor"),
        ),
        out_specs=(
            P(None, "tensor"),
            P("dp", None, "tensor"),
            P("dp", None, "tensor"),
            P("dp", None, "tensor"),
        ),
        check_vma=False,
    )
```

```python
import functools

import jax
import jax.numpy as jnp
from jax import lax
from jax.experimental import pallas as pl
from jax.experimental.pallas import tpu as pltpu
from jax.sharding import PartitionSpec as P

beta_first = 0.9
beta_second = 0.95
learn_rate = 0.001
adam_eps = 1e-08
adam_step = 100.0

MESH = pl.DeviceIdType.MESH
TOK = 384
FEAT = 832
HD = 128
NBLK = 52
HALF = 26
HROWS = HALF * 128
SUB = 16
OWN = 7
PAD = 8 * OWN
CHUNKS = 3
CTOK = TOK // CHUNKS
LEVELS = 32700.0
FINE = 8388000.0
FIXED = 32766.0
TOP_MASTER = 0.078125
TOP_FIRST = 4.0
TOP_SECOND = 1.0


def adam_update(gradient, master, first, second, used):
    first_new = beta_first * first + (1.0 - beta_first) * gradient
    second_new = beta_second * second + (1.0 - beta_second) * gradient * gradient
    corr_first = 1.0 - beta_first**adam_step
    corr_second = 1.0 - beta_second**adam_step
    master_new = master - learn_rate * (first_new / corr_first) / (
        jnp.sqrt(second_new / corr_second) + adam_eps
    )
    return (master_new * used, first_new * used, second_new * used)


def dot_t(a, b):
    return lax.dot_general(a, b, (((1,), (1,)), ((), ())), preferred_element_type=jnp.float32)


def dot_0(a, b):
    return lax.dot_general(a, b, (((0,), (0,)), ((), ())), preferred_element_type=jnp.float32)


def pack(v, inv):
    q = jnp.round(v * inv).astype(jnp.int32)
    k = q.shape[0] // 2
    return (q[:k] << 16) | (q[k:] & 0xFFFF)


def unpack(u, step):
    return jnp.concatenate([u >> 16, (u << 16) >> 16], axis=0).astype(jnp.float32) * step


def pack_fine(v, inv):
    q = jnp.round(v * inv).astype(jnp.int32)
    last = q[96:]
    return jnp.concatenate(
        [
            (q[0:32] << 8) | (last & 255),
            (q[32:64] << 8) | ((last >> 8) & 255),
            (q[64:96] << 8) | ((last >> 16) & 255),
        ],
        axis=0,
    )


def unpack_fine(u, step):
    last = ((u[64:96] << 24) >> 8) | ((u[32:64] & 255) << 8) | (u[0:32] & 255)
    return jnp.concatenate([u >> 8, last], axis=0).astype(jnp.float32) * step


def level(top):
    bits = jnp.log(jnp.maximum(top, 1e-30)) * (8.0 / 0.6931471805599453)
    return jnp.ceil(bits).astype(jnp.int32)


def step_of(e):
    return jnp.exp(e.astype(jnp.float32) * (0.6931471805599453 / 8.0)) * (1.0 / LEVELS)


def inverse_of(e):
    return jnp.exp(e.astype(jnp.float32) * (-0.6931471805599453 / 8.0)) * LEVELS


def kernel(
    slot_code, block_code,
    act, w, keys, values, outg, master, first, second,
    wst, recv_g,
    whole, sib, wt, wo, qo, po, pr, pm, pn, dqs, dqa, grad, ys, yr, gsum, zs, zr, red, gq,
    sys, syr, szs, szr, send_g,
    x_s, x_r, f_s, f_r, s_s, s_r, b_s, b_r, e_s, e_r, q_s, q_r, n_s, n_r, h_s, h_r, d_s, d_r, y_s, y_r, r_s, r_r,
    a_s, a_r, o_s, o_r, w_s, w_r, v_s, v_r, c_s, c_r, k_s, k_r, p_s, p_r, l_sem,
):
    dp = lax.axis_index("dp")
    t = lax.axis_index("tensor")
    zl = dp // 8
    part = lax.rem(dp, 8)
    y = part // 2
    c = lax.rem(part, 2)
    a = t // 4
    x = lax.rem(t, 4)
    f32 = jnp.float32
    bf16 = jnp.bfloat16

    def device(z, y, c, a):
        return (z * 8 + y * 2 + c, a * 4 + x)

    def at_x(d):
        return (dp, a * 4 + lax.rem(x + d, 4))

    def at_part(p):
        return (zl * 8 + p, t)

    def at_z(z):
        return (z * 8 + part, t)

    opposite = device(zl, y, c, 1 - a)
    sibling = device(zl, y, 1 - c, a)

    def rows(start, n, unit):
        return pl.ds(pl.multiple_of(start, unit), n)

    barrier = pltpu.get_barrier_semaphore()
    peers = [at_x(d) for d in (1, 2, 3)] + [opposite]
    peers += [at_part(lax.rem(part + d, 8)) for d in range(1, 8)]
    peers += [at_z(lax.rem(zl + d, 8)) for d in range(1, 8)]
    peers += [device(lax.rem(zl + d, 8), y, 1 - c, 1 - a) for d in range(8)]
    for peer in peers:
        pl.semaphore_signal(barrier, inc=1, device_id=peer, device_id_type=MESH)

    def turn(k, carry):
        r = rows(k * 128, 128, 128)
        wt[r, 0:128] = w[k * 2].astype(f32).T.astype(bf16)
        wt[r, 128:256] = w[k * 2 + 1].astype(f32).T.astype(bf16)
        return carry

    lax.fori_loop(0, HALF, turn, 0)

    def states(p, carry):
        for j in range(2):
            for s in range(2):
                r = rows((p // 2) * 32 + s * SUB, SUB, SUB)
                n = j * 2 + s
                sys[p, n] = pack(master[j, r], FIXED / TOP_MASTER)
                sys[p, 4 + n] = pack(first[j, r], FIXED / TOP_FIRST)
                sys[p, 8 + n] = pack(second[j, r], FIXED / TOP_SECOND)
        return carry

    lax.fori_loop(0, 8, states, 0)
    pl.semaphore_wait(barrier, len(peers))
    sent = []

    def copy(src, dst, ss, rs, dev):
        return pltpu.make_async_remote_copy(
            src_ref=src, dst_ref=dst, send_sem=ss, recv_sem=rs, device_id=dev, device_id_type=MESH
        )

    def go(src, dst, ss, rs, dev):
        cp = copy(src, dst, ss, rs, dev)
        cp.start()
        sent.append(cp)
        return cp

    eighth = rows(part * 208, 208, 16)
    odd = lax.rem(zl, 2)
    lanes = [rows(odd * 128, 128, 128), rows((1 - odd) * 128, 128, 128)]
    w_cross = go(
        wt.at[rows((1 - a) * (HROWS // 2) + part * 208, 208, 16), lanes[0]], wo.at[eighth, lanes[0]],
        b_s.at[0], b_r.at[0], opposite,
    )

    cols = [pl.ds(i * CTOK, CTOK) for i in range(CHUNKS)]
    mine = rows(x * FEAT, FEAT, 16)
    own = pltpu.make_async_copy(act, whole.at[mine], l_sem)
    own.start()
    order = (2, 1, 0)
    along = {
        i: [
            go(act.at[:, cols[i]], whole.at[mine, cols[i]], x_s.at[n, i], x_r.at[n, i], at_x(d))
            for n, d in enumerate((1, 3))
        ]
        for i in order
    }
    onward = {}

    def pass_on(i):
        onward[i] = []
        for n, d in enumerate((1, 3)):
            along[i][n].wait_recv()
            r = rows(lax.rem(x - d + 4, 4) * FEAT + n * 416, 416, 16)
            at = whole.at[r, cols[i]]
            onward[i].append(go(at, at, f_s.at[n, i], f_r.at[n, i], at_x(d)))

    state_y = []
    for d in range(1, 8):
        p = lax.rem(part + d, 8)
        state_y.append(
            go(sys.at[p], syr.at[pl.ds(part * 12, 12)], k_s.at[d - 1], k_r.at[d - 1], at_part(p))
        )
    syr[pl.ds(part * 12, 12)] = sys[part]
    for cp in state_y:
        cp.wait_recv()

    def states_z(z, carry):
        for j in range(OWN):
            u = z * OWN + j
            at = (block_code[jnp.minimum(c * HALF + u // 2, NBLK - 1)] & 127) + lax.rem(u, 2)
            for m in range(3):
                szs[m, z, j] = syr[at + 4 * m]
        return carry

    lax.fori_loop(0, 8, states_z, 0)
    state_z = []

    def send_states(m):
        szr[m, pl.ds(zl * OWN, OWN)] = szs[m, zl]
        for d in range(1, 8):
            z = lax.rem(zl + d, 8)
            state_z.append(
                go(
                    szs.at[m, z], szr.at[m, pl.ds(zl * OWN, OWN)],
                    p_s.at[m, d - 1], p_r.at[m, d - 1], at_z(z),
                )
            )

    send_states(0)
    send_states(1)
    pass_on(2)
    w_cross.wait_recv()
    at = wo.at[eighth, lanes[0]]
    w_next = go(at, at, e_s.at[0], e_r.at[0], at_z(zl + 1 - 2 * odd))
    w_part = []

    def spread(n, ss, rs):
        at = wo.at[eighth, lanes[n]]
        for d in range(1, 8):
            w_part.append(go(at, at, ss.at[d], rs.at[d], at_part(lax.rem(part + d, 8))))

    spread(0, b_s, b_r)
    w_next.wait_recv()
    spread(1, e_s, e_r)
    pass_on(1)
    pass_on(0)

    def partial(weights, first_row, i):
        total = jnp.zeros((HD, CTOK), f32)
        for n in range(13):
            total = total + jnp.dot(
                weights[rows(first_row + n * 128, 128, 128)],
                whole[pl.ds(n * 256, 256), cols[i]],
                preferred_element_type=f32,
            )
        return total

    own.wait()
    share = []
    q_cross = {}
    grad[pl.ds(HROWS, 256)] = jnp.zeros((256, HD), f32)
    for i in order:
        for cp in onward[i]:
            cp.wait_recv()
        share.append(go(whole.at[:, cols[i]], sib.at[:, cols[i]], s_s.at[i], s_r.at[i], sibling))
        if i == order[0]:
            qo[i] = partial(wt, a * (HROWS // 2), i)
            for cp in w_part:
                cp.wait_recv()
        other = partial(wo, 0, i)
        top = jnp.maximum(jnp.max(jnp.abs(other), axis=0, keepdims=True), 1e-30)
        po[i] = pack_fine(other, FINE / top)
        pm[i] = jnp.broadcast_to(top, (8, CTOK))
        q_cross[i] = [
            go(pm.at[i], pn.at[i], n_s.at[i], n_r.at[i], opposite),
            go(po.at[i], pr.at[i], q_s.at[i], q_r.at[i], opposite),
        ]
    for i in order[1:]:
        qo[i] = partial(wt, a * (HROWS // 2), i)

    factor = HD ** (-0.5)
    same = a == c
    dq_cross = []
    for i in order:
        for cp in q_cross[i]:
            cp.wait_recv()
        other = unpack_fine(pr[i], pn[i, 0:1] * (1.0 / FINE))
        queries = (qo[i] + other).T.astype(bf16)
        n = (i + 1) * CTOK
        kk = keys[pl.ds(0, n)]
        vv = values[pl.ds(0, n)]
        og = outg[cols[i]]
        scores = dot_t(queries, kk) * factor
        row_pos = lax.broadcasted_iota(jnp.int32, (CTOK, n), 0) + i * CTOK
        col_pos = lax.broadcasted_iota(jnp.int32, (CTOK, n), 1)
        scores = jnp.where(row_pos >= col_pos, scores, -1e30)
        shifted = jnp.exp(scores - jnp.max(scores, axis=1, keepdims=True))
        attention = shifted / jnp.sum(shifted, axis=1, keepdims=True)
        outputs = jnp.dot(attention.astype(bf16), vv, preferred_element_type=f32)
        deltas = jnp.sum(og.astype(f32) * outputs, axis=1, keepdims=True)
        upstream = dot_t(og, vv)
        dscores = (attention * (upstream - deltas)).astype(bf16)
        dquery = jnp.dot(dscores, kk, preferred_element_type=f32) * factor
        dqs[cols[i]] = dquery.astype(bf16)
        go(
            dqs.at[cols[i]], dqa.at[c, cols[i]], d_s.at[i], d_r.at[i, c], device(zl, y, a, 1 - a)
        )

        @pl.when(same)
        def _():
            dqa[c, cols[i]] = dqs[cols[i]]

        @pl.when(jnp.logical_not(same))
        def _():
            copy(dqs.at[cols[i]], dqa.at[c, cols[i]], h_s.at[i], h_r.at[i], sibling).start()

    send_states(2)

    def wait_dq(i):
        @pl.when(same)
        def _():
            copy(dqs.at[cols[i]], dqa.at[1 - c, cols[i]], h_s.at[i], h_r.at[i], sibling).wait_recv()

        @pl.when(jnp.logical_not(same))
        def _():
            for s in range(2):
                copy(
                    dqs.at[cols[i]], dqa.at[s, cols[i]], d_s.at[i], d_r.at[i, s], opposite
                ).wait_recv()
            copy(dqs.at[cols[i]], dqa.at[c, cols[i]], h_s.at[i], h_r.at[i], sibling).wait_send()

    def add_grad(lo, n, fresh):
        tok = pl.ds(lo, n)

        def one(j, top):
            r = rows(j * FEAT, FEAT, 16)
            g = jnp.dot(whole[r, tok], dqa[c, tok], preferred_element_type=f32)
            g = g + jnp.dot(sib[r, tok], dqa[1 - c, tok], preferred_element_type=f32)
            if not fresh:
                g = g + grad[r]
            grad[r] = g
            return jnp.maximum(top, jnp.max(jnp.abs(g), axis=0, keepdims=True))

        return lax.fori_loop(0, 4, one, jnp.zeros((1, HD), f32))

    for cp in share:
        cp.wait_recv()
    wait_dq(2)
    wait_dq(1)
    add_grad(CTOK, 2 * CTOK, True)
    wait_dq(0)
    top = add_grad(0, CTOK, False)

    e = jnp.broadcast_to(level(top), (8, HD))
    inv = inverse_of(e[:1])
    to_y = []
    for h in range(2):

        def to_fixed(k, carry):
            for j in range(OWN):
                u = (2 * k + h) * OWN + j
                r = (u // 2) * 128 + lax.rem(u, 2) * SUB
                for p in range(4):
                    ys[h, p, k * OWN + j] = pack(grad[rows(r + p * 32, SUB, SUB)], inv)
            return carry

        lax.fori_loop(0, 4, to_fixed, 0)
        for p in range(4):
            ys[h, p, 4 * OWN] = e
        for d in (1, 3, 2):
            p = lax.rem(y + d, 4)
            to_y.append(
                go(ys.at[h, p], yr.at[h, y], y_s.at[h, d - 1], y_r.at[h, d - 1], device(zl, p, c, a))
            )
        yr[h, y] = ys[h, y]

    def to_place(z):
        return copy(zs.at[z], zr.at[zl], r_s.at[z], r_r.at[zl], device(z, y, a, c))

    def from_place(z):
        return copy(zs.at[z], zr.at[z], r_s.at[z], r_r.at[z], device(z, y, a, c))

    def stays(z):
        return jnp.logical_and(same, zl == z)

    for h in range(2):
        for cp in to_y[3 * h : 3 * h + 3]:
            cp.wait_recv()
        steps = [step_of(yr[h, p, 4 * OWN, 0:1]) for p in range(4)]

        def add_y(k, carry):
            for j in range(OWN):
                u = k * OWN + j
                total = unpack(yr[h, 0, u], steps[0])
                for p in range(1, 4):
                    total = total + unpack(yr[h, p, u], steps[p])
                gsum[u] = total
            return carry

        lax.fori_loop(0, 4, add_y, 0)
        e = jnp.broadcast_to(level(LEVELS * (steps[0] + steps[1] + steps[2] + steps[3])), (8, HD))
        inv = inverse_of(e[:1])

        def to_fixed_z(k, carry):
            for j in range(OWN):
                zs[2 * k + h, j] = pack(gsum[k * OWN + j], inv)
            zs[2 * k + h, OWN] = e
            return carry

        lax.fori_loop(0, 4, to_fixed_z, 0)
        for k in range(4):
            z = 2 * k + h

            @pl.when(stays(z))
            def _():
                zr[zl] = zs[z]

            @pl.when(jnp.logical_not(stays(z)))
            def _():
                to_place(z).start()

    for z in range(8):

        @pl.when(jnp.logical_not(stays(z)))
        def _():
            from_place(z).wait_recv()

    for cp in state_z:
        cp.wait_recv()
    steps = [step_of(zr[z, OWN, 0:1]) for z in range(8)]
    for j in range(OWN):
        total = unpack(zr[0, j], steps[0])
        for z in range(1, 8):
            total = total + unpack(zr[z, j], steps[z])
        red[j] = total
        u = zl * OWN + j
        at = (block_code[jnp.minimum(c * HALF + u // 2, NBLK - 1)] >> 7) + j
        m_state = unpack(szr[0, at], TOP_MASTER / FIXED)
        f_state = unpack(szr[1, at], TOP_FIRST / FIXED)
        s_state = unpack(szr[2, at], TOP_SECOND / FIXED)
        nm, _, _ = adam_update(total, m_state, f_state, s_state, 1.0)
        wst[part, u] = nm.astype(bf16)

    def weights(z, p):
        return wst.at[p, pl.ds(z * OWN, OWN)]

    w_z = []
    for d in range(1, 8):
        z = lax.rem(zl + d, 8)
        w_z.append(go(weights(zl, part), weights(zl, part), w_s.at[d - 1], w_r.at[d - 1], at_z(z)))
    bound = steps[0]
    for z in range(1, 8):
        bound = bound + steps[z]
    e = level(LEVELS * bound)
    inv = inverse_of(e)
    g_step = step_of(e)
    for j in range(OWN):
        gq[zl * OWN + j] = pack(red[j], inv)
    g_z = []
    for d in range(1, 8):
        z = lax.rem(zl + d, 8)
        at = gq.at[pl.ds(zl * OWN, OWN)]
        g_z.append(go(at, at, a_s.at[d - 1], a_r.at[d - 1], at_z(z)))

    back_y = []
    to_core = []
    for d in range(8):
        z = lax.rem(zl - d + 8, 8)
        if d:
            w_z[d - 1].wait_recv()
        at = weights(z, part)
        back_y.append(
            [
                go(at, at, v_s.at[q - 1, d], v_r.at[q - 1, d], device(zl, lax.rem(y + q, 4), c, a))
                for q in (1, 3, 2)
            ]
        )
        to_core.append(go(at, at, c_s.at[0, d], c_r.at[0, d], sibling))

    for cp in g_z:
        cp.wait_recv()
    for p in range(8):
        for j in range(2):
            code = slot_code[zl * 16 + p * 2 + j]
            for s in range(2):
                u = (code >> (6 * s)) & 63
                send_g[p, j * 2 + s] = unpack(gq[u], g_step)
    to_owner = []
    for d in range(1, 8):
        p = lax.rem(part + d, 8)
        to_owner.append(
            go(send_g.at[p], recv_g.at[pl.ds(part * 4, 4)], o_s.at[d - 1], o_r.at[d - 1], at_part(p))
        )
    recv_g[pl.ds(part * 4, 4)] = send_g[part]
    for d in range(8):
        z = lax.rem(zl - d + 8, 8)
        for n, q in enumerate((1, 3, 2)):
            back_y[d][n].wait_recv()
            at = weights(z, lax.rem(y - q + 4, 4) * 2 + c)
            to_core.append(go(at, at, c_s.at[q, d], c_r.at[q, d], sibling))
    for cp in to_owner:
        cp.wait_recv()
    for cp in to_core:
        cp.wait_recv()

    for z in range(8):

        @pl.when(jnp.logical_not(stays(z)))
        def _():
            to_place(z).wait_send()

    for cp in sent:
        cp.wait_send()


def finish(slot_code, parts, recv, master, first, second, out_w, out_m, out_f, out_s, recv_g, held, sem):
    moves = [pltpu.make_async_copy(recv, recv_g, sem.at[8])]
    for p in range(8):
        moves.append(pltpu.make_async_copy(parts.at[p], held.at[p], sem.at[p]))
    for cp in moves:
        cp.start()
    moves[0].wait()
    for j in range(2):
        code = slot_code[lax.axis_index("dp") * 2 + j]
        used = (code >> 13).astype(jnp.float32)
        h = ((code >> 12) & 1) * 4
        for n in range(4):
            for s in range(2):
                g = recv_g[h + (n * 8 + j * 2 + s)]
                r = pl.ds(n * 32 + s * SUB, SUB)
                nm, nf, ns = adam_update(g, master[j, r], first[j, r], second[j, r], used)
                out_m[j, r] = nm
                out_f[j, r] = nf
                out_s[j, r] = ns
    for p in range(8):
        moves[1 + p].wait()
        b = (p % 2) * HALF
        r = (p // 2) * 32
        out_w[b : b + HALF, r : r + 32] = held[p, 0:HALF]


def body(
    activation, w_query, key_rows, value_rows, out_grad, owners, master_copy, first_moment, second_moment
):
    own_row = owners[0, :, 0]
    order = jnp.arange(NBLK, dtype=jnp.int32)
    earlier = (own_row[:, None] == own_row[None, :]) & (order[:, None] < order[None, :])
    second_slot = jnp.sum(earlier.astype(jnp.int32), axis=0)
    target = own_row * 2 + second_slot
    match = target[None, :] == jnp.arange(128, dtype=jnp.int32)[:, None]
    unit = (order % HALF) * 2
    place = unit
    place = place + 64 * (unit + 1)
    place = place + 4096 * (order // HALF) + 8192
    slot_code = jnp.sum(jnp.where(match, place[None, :], 0), axis=1)
    block_code = (own_row >> 3) * (OWN * 128) + (own_row & 7) * 12 + second_slot * 2
    smem = pl.BlockSpec(memory_space=pltpu.SMEM)
    vmem = pl.BlockSpec(memory_space=pltpu.VMEM)
    anywhere = pl.BlockSpec(memory_space=pl.ANY)
    f32 = jnp.float32
    bf16 = jnp.bfloat16
    i32 = jnp.int32
    dma = pltpu.SemaphoreType.DMA

    def pair(*dims):
        return [dma(dims), dma(dims)]

    parts, gradient = pl.pallas_call(
        kernel,
        out_shape=(
            jax.ShapeDtypeStruct((8, PAD, SUB, HD), bf16),
            jax.ShapeDtypeStruct((32, SUB, HD), f32),
        ),
        in_specs=[smem] * 2 + [vmem] * 8,
        out_specs=(vmem,) * 2,
        scratch_shapes=[
            pltpu.VMEM((HROWS, TOK), bf16),
            pltpu.VMEM((HROWS, TOK), bf16),
            pltpu.VMEM((HROWS, 256), bf16),
            pltpu.VMEM((HROWS // 2, 256), bf16),
            pltpu.VMEM((CHUNKS, HD, CTOK), f32),
            pltpu.VMEM((CHUNKS, 96, CTOK), i32),
            pltpu.VMEM((CHUNKS, 96, CTOK), i32),
            pltpu.VMEM((CHUNKS, 8, CTOK), f32),
            pltpu.VMEM((CHUNKS, 8, CTOK), f32),
            pltpu.VMEM((TOK, HD), bf16),
            pltpu.VMEM((2, TOK, HD), bf16),
            pltpu.VMEM((HROWS + 256, HD), f32),
            pltpu.VMEM((2, 4, 4 * OWN + 1, 8, HD), i32),
            pltpu.VMEM((2, 4, 4 * OWN + 1, 8, HD), i32),
            pltpu.VMEM((4 * OWN, SUB, HD), f32),
            pltpu.VMEM((8, OWN + 1, 8, HD), i32),
            pltpu.VMEM((8, OWN + 1, 8, HD), i32),
            pltpu.VMEM((OWN, SUB, HD), f32),
            pltpu.VMEM((PAD, 8, HD), i32),
            pltpu.VMEM((8, 12, 8, HD), i32),
            pltpu.VMEM((96, 8, HD), i32),
            pltpu.VMEM((3, 8, OWN, 8, HD), i32),
            pltpu.VMEM((3, PAD, 8, HD), i32),
            pltpu.VMEM((8, 4, SUB, HD), f32),
        ]
        + pair(2, CHUNKS)
        + pair(2, CHUNKS)
        + pair(CHUNKS)
        + pair(8)
        + pair(8)
        + pair(CHUNKS)
        + pair(CHUNKS)
        + pair(CHUNKS)
        + [dma((CHUNKS,)), dma((CHUNKS, 2))]
        + pair(2, 3)
        + pair(8)
        + pair(7)
        + pair(7)
        + pair(7)
        + pair(3, 8)
        + pair(4, 8)
        + pair(7)
        + pair(3, 7)
        + [dma],
        compiler_params=pltpu.CompilerParams(
            collective_id=0, has_side_effects=True, vmem_limit_bytes=56 * 2**20
        ),
        name="project_back",
    )(
        slot_code, block_code,
        activation.T, w_query.reshape(NBLK, 128, HD), key_rows, value_rows, out_grad,
        master_copy, first_moment, second_moment,
    )
    new_w, new_m, new_f, new_s = pl.pallas_call(
        finish,
        out_shape=(
            jax.ShapeDtypeStruct((NBLK, 128, HD), bf16),
            jax.ShapeDtypeStruct((2, 128, HD), f32),
            jax.ShapeDtypeStruct((2, 128, HD), f32),
            jax.ShapeDtypeStruct((2, 128, HD), f32),
        ),
        in_specs=[smem, anywhere, anywhere] + [vmem] * 3,
        out_specs=(vmem,) * 4,
        scratch_shapes=[
            pltpu.VMEM((32, SUB, HD), f32),
            pltpu.VMEM((8, PAD // 2, 2 * SUB, HD), bf16),
            dma((9,)),
        ],
        compiler_params=pltpu.CompilerParams(vmem_limit_bytes=56 * 2**20),
        name="finish",
    )(slot_code, parts.reshape(8, PAD // 2, 2 * SUB, HD), gradient, master_copy, first_moment, second_moment)
    return (new_w.reshape(NBLK * 128, HD), new_m, new_f, new_s)


def solution(mesh):
    return jax.shard_map(
        body,
        mesh=mesh,
        in_specs=(
            P("dp", "tensor"),
            P(None, "tensor"),
            P("dp", "tensor"),
            P("dp", "tensor"),
            P("dp", "tensor"),
            P("tensor", None, None),
            P("dp", None, "tensor"),
            P("dp", None, "tensor"),
            P("dp", None, "tensor"),
        ),
        out_specs=(
            P(None, "tensor"),
            P("dp", None, "tensor"),
            P("dp", None, "tensor"),
            P("dp", None, "tensor"),
        ),
        check_vma=False,
    )
```
